256 devices in a mesh: section: 2 (over y_lo), azim: 32 (over x, z), axial: 4 (over y_hi, core).
Axes of the slice: x: 4, y: 4 (y_hi: 2, y_lo: 2; y = y_hi * 2 + y_lo), z: 8, core: 2. Of those that a mesh axis runs over, the one named last changes fastest.
Arguments:
- magnetic_vector_field: float32 [3, 32, 512, 512], P(None, 'azim', 'section', 'axial'), may hold values from -3 to 3
- imposed_current_density: float32 [3, 32, 512, 512], P(None, 'azim', 'section', 'axial'), may hold values from -6 to 6
- fixed_material_map: int32 [32, 512, 512], P('azim', 'section', 'axial'), may hold values from 0 to 7
- spinning_material_map: int32 [32, 128], replicated, may hold values from 0 to 7
- slab_slide_offsets: int32 [512], P('axial'), may hold values from 0 to 31, as said below
- inverse_permeability: float32 [8], replicated, may hold values from 0.1 to 1
- electric_conductance: float32 [8], replicated, may hold values from 0.05 to 0.5
- core_dissipation_coefficient: float32 [8], replicated, may hold values from 0.2 to 2
- inplane_thermal_conductance: float32 [8], replicated, may hold values from 1 to 4
- through_plane_conductance: float32 [8], replicated, may hold values from 0.1 to 0.5
- thermal_storage: float32 [8], replicated, may hold values from 0.05 to 0.3
- prior_thermal_state: float32 [32, 512, 512], P(None, ('section', 'azim'), 'axial'), may hold values from -6 to 6
- goal_sensitivity: float32 [32, 512, 512], P(None, ('section', 'azim'), 'axial'), may hold values from -16 to 16
Outputs:
- magnetic_misfit: float32 [3, 32, 512, 512], P(None, 'azim', 'section', 'axial')
- dual_magnetic_rhs: float32 [3, 32, 512, 512], P(None, 'azim', 'section', 'axial')
- thermal_state: float32 [32, 512, 512], P('azim', 'section', 'axial')
The draws below stay inside these ranges and needn't reach their ends.
Inputs may be any that keep to these rules, and one draw needn't show every extreme that they name: `slab_slide_offsets`: the smallest and the largest offset each occur at some layer.
All inputs are finite; a program needn't handle non-finite values.
Results may differ from the reference program's by a relative error of at most 0.00002.
Values sent between devices are 32-bit elements; how exact they have to be, the bound alone decides.
No kernel may reach another device: no remote copies, remote signals or barrier semaphores. Data moves between devices by JAX's collectives and lax.ppermute only.
A program may use at most 64 MiB of HBM per device.

```python
import math
import jax
import jax.numpy as jnp

NREG = 8
SWEEPS = 4
ANGULAR_BINS = 32
RADIUS_BINS = 512
LENGTHWISE_SLABS = 512
RROT = 128


def draw_slab_slide_offsets(key, part):
    first, second = jax.random.split(jax.random.fold_in(key, 11))
    offsets = jax.random.randint(first, (LENGTHWISE_SLABS,), 0, ANGULAR_BINS)
    places = jax.random.permutation(second, LENGTHWISE_SLABS)
    offsets = offsets.at[places[0]].set(0)
    offsets = offsets.at[places[1]].set(ANGULAR_BINS - 1)
    return offsets.astype(jnp.int32)


def draw_goal_sensitivity(key, part):
    shape = (ANGULAR_BINS, RADIUS_BINS, LENGTHWISE_SLABS)
    return jnp.clip(4.0 * jax.random.normal(key, shape, jnp.float32), -16.0, 16.0)


def set_ends(drawn, own_key, low, largest):
    place = [jax.random.randint(jax.random.fold_in(own_key, axis), (), 0, length) for axis, length in enumerate(drawn.shape)]
    main_axis = drawn.shape.index(max(drawn.shape))
    beside = place[:main_axis] + [(place[main_axis] + 1) % drawn.shape[main_axis]] + place[main_axis + 1:]
    return drawn.at[tuple(place)].set(low).at[tuple(beside)].set(largest)


def block_scale(own_key, extent, cuts, least, high):
    def one(axis_at, blocks):
        steps = jax.random.uniform(jax.random.fold_in(jax.random.fold_in(own_key, 6), axis_at), (blocks,), jnp.float32, least / len(cuts), high / len(cuts))
        return jnp.repeat(jnp.exp(steps), extent[axis_at] // blocks).reshape((-1,) + (1,) * (len(extent) - axis_at - 1))

    level = one(*cuts[0])
    for cut in cuts[1:]:
        level = level * one(*cut)
    return level


def centred(key, dims, width, limit, cuts=(), kind=jnp.bfloat16):
    level = block_scale(key, dims, cuts, -0.22, 0.18) if cuts else 1.0
    values = jax.random.normal(key, dims, jnp.float32) * width * level
    return jnp.minimum(jnp.maximum(values, -limit), limit).astype(kind)


def setup_inputs(seed: int = 0) -> dict:
    key_list = jax.random.split(jax.random.key(seed), 14)
    magnetic_vector_field = centred(key_list[0], (3, ANGULAR_BINS, RADIUS_BINS, LENGTHWISE_SLABS), 0.5, 3.0, ((1, 32), (2, 2), (3, 4)), jnp.float32)
    imposed_current_density = centred(key_list[1], (3, ANGULAR_BINS, RADIUS_BINS, LENGTHWISE_SLABS), 1.0, 6.0, ((1, 32), (2, 2), (3, 4)), jnp.float32)
    fixed_material_map = set_ends(jax.random.randint(key_list[2], (ANGULAR_BINS, RADIUS_BINS, LENGTHWISE_SLABS), 0, NREG), jax.random.fold_in(key_list[2], 1), 0, NREG - 1).astype(jnp.int32)
    spinning_material_map = set_ends(jax.random.randint(key_list[3], (ANGULAR_BINS, RROT), 0, NREG), jax.random.fold_in(key_list[3], 1), 0, NREG - 1).astype(jnp.int32)
    slab_slide_offsets = draw_slab_slide_offsets(jax.random.fold_in(key_list[13], 71), 0)
    inverse_permeability = jnp.clip(jnp.exp(jax.random.uniform(key_list[5], (NREG,), jnp.float32, math.log(0.1), math.log(1.0))), 0.1, 1.0)
    electric_conductance = jnp.clip(jnp.exp(jax.random.uniform(key_list[6], (NREG,), jnp.float32, math.log(0.05), math.log(0.5))), 0.05, 0.5)
    core_dissipation_coefficient = jnp.clip(jnp.exp(jax.random.uniform(key_list[7], (NREG,), jnp.float32, math.log(0.2), math.log(2.0))), 0.2, 2.0)
    inplane_thermal_conductance = jnp.clip(jnp.exp(jax.random.uniform(key_list[8], (NREG,), jnp.float32, math.log(1.0), math.log(4.0))), 1.0, 4.0)
    through_plane_conductance = jnp.clip(jnp.exp(jax.random.uniform(key_list[9], (NREG,), jnp.float32, math.log(0.1), math.log(0.5))), 0.1, 0.5)
    thermal_storage = jnp.clip(jnp.exp(jax.random.uniform(key_list[10], (NREG,), jnp.float32, math.log(0.05), math.log(0.3))), 0.05, 0.3)
    prior_thermal_state = centred(key_list[11], (ANGULAR_BINS, RADIUS_BINS, LENGTHWISE_SLABS), 1.0, 6.0, ((1, 64), (2, 4)), jnp.float32)
    goal_sensitivity = draw_goal_sensitivity(jax.random.fold_in(key_list[13], 71), 0)
    return {"magnetic_vector_field": magnetic_vector_field, "imposed_current_density": imposed_current_density, "fixed_material_map": fixed_material_map, "spinning_material_map": spinning_material_map, "slab_slide_offsets": slab_slide_offsets, "inverse_permeability": inverse_permeability, "electric_conductance": electric_conductance, "core_dissipation_coefficient": core_dissipation_coefficient, "inplane_thermal_conductance": inplane_thermal_conductance, "through_plane_conductance": through_plane_conductance, "thermal_storage": thermal_storage, "prior_thermal_state": prior_thermal_state, "goal_sensitivity": goal_sensitivity}


def region_map(fixed_material_map, spinning_material_map, slab_slide_offsets, azim_cells, radial_cells, azim_total):
    shifted = jnp.mod(azim_cells[:, None] - slab_slide_offsets[None, :], azim_total).astype(jnp.int32)
    rotor_rows = jnp.transpose(spinning_material_map[shifted], (0, 2, 1))
    extra = fixed_material_map.shape[1] - rotor_rows.shape[1]
    rotor_rows = jnp.pad(rotor_rows, ((0, 0), (0, extra), (0, 0)))
    inside = (radial_cells < spinning_material_map.shape[1])[None, :, None]
    return jnp.where(inside, rotor_rows, fixed_material_map)


def lookup(regions, materials):
    results = [jnp.zeros(regions.shape, jnp.float32) for material in materials]
    for region in range(NREG):
        matches = regions == region
        results = [jnp.where(matches, material[region], result) for material, result in zip(materials, results)]
    return results


def forward_diff(values, axis_dim):
    difference = jnp.diff(values, axis=axis_dim)
    window = [slice(0, -1), slice(0, -1), slice(0, -1)]
    window[axis_dim] = slice(None)
    return difference[tuple(window)]


def backward_diff(values, axis_dim):
    difference = -jnp.diff(values, axis=axis_dim)
    window = [slice(1, None), slice(1, None), slice(1, None)]
    window[axis_dim] = slice(None)
    return difference[tuple(window)]


def em_terms(padded):
    azim_part, radial_part, axial_part, reluct_pad = padded[0], padded[1], padded[2], padded[3]
    flux_azim = forward_diff(axial_part, 1) - forward_diff(radial_part, 2)
    flux_radial = forward_diff(azim_part, 2) - forward_diff(axial_part, 0)
    flux_axial = forward_diff(radial_part, 0) - forward_diff(azim_part, 1)
    reluct_cell = reluct_pad[:-1, :-1, :-1]
    field_azim = reluct_cell * flux_azim
    field_radial = reluct_cell * flux_radial
    field_axial = reluct_cell * flux_axial
    curl_azim = backward_diff(field_radial, 2) - backward_diff(field_axial, 1)
    curl_radial = backward_diff(field_axial, 0) - backward_diff(field_azim, 2)
    curl_axial = backward_diff(field_azim, 1) - backward_diff(field_radial, 0)
    curl_term = jnp.stack([curl_azim, curl_radial, curl_axial])
    flux = jnp.stack([flux_azim, flux_radial, flux_axial])[:, 1:, 1:, 1:]
    return curl_term, flux


def relax(padded, local_thermal_storage, right_hand_sides):
    interior = padded[:, :, 1:-1, 1:-1]
    repeat_relaxation_passes = interior[:2]
    plane_cell = interior[2]
    axial_cell = interior[3]
    faces = [
        (jnp.roll(repeat_relaxation_passes, -1, axis=1), jnp.roll(plane_cell, -1, axis=0), plane_cell),
        (jnp.roll(repeat_relaxation_passes, 1, axis=1), jnp.roll(plane_cell, 1, axis=0), plane_cell),
        (padded[:2, :, 2:, 1:-1], padded[2, :, 2:, 1:-1], plane_cell),
        (padded[:2, :, :-2, 1:-1], padded[2, :, :-2, 1:-1], plane_cell),
        (padded[:2, :, 1:-1, 2:], padded[3, :, 1:-1, 2:], axial_cell),
        (padded[:2, :, 1:-1, :-2], padded[3, :, 1:-1, :-2], axial_cell),
    ]
    weight_sum = jnp.zeros(plane_cell.shape, jnp.float32)
    inflow = jnp.zeros(repeat_relaxation_passes.shape, jnp.float32)
    for neighbour, beside, own in faces:
        weight = 0.5 * (own + beside)
        weight_sum = weight_sum + weight
        inflow = inflow + weight * neighbour
    return (right_hand_sides + inflow) / (local_thermal_storage + weight_sum)


def pad_grid(stacked):
    wrapped = jnp.concatenate([stacked[:, -1:], stacked, stacked[:, :1]], axis=1)
    return jnp.pad(wrapped, ((0, 0), (0, 0), (1, 1), (1, 1)))


def reference(magnetic_vector_field, imposed_current_density, fixed_material_map, spinning_material_map, slab_slide_offsets, inverse_permeability, electric_conductance, core_dissipation_coefficient, inplane_thermal_conductance, through_plane_conductance, thermal_storage, prior_thermal_state, goal_sensitivity):
    azim_cells = jnp.arange(ANGULAR_BINS, dtype=jnp.int32)
    radial_cells = jnp.arange(RADIUS_BINS, dtype=jnp.int32)
    regions = region_map(fixed_material_map, spinning_material_map, slab_slide_offsets, azim_cells, radial_cells, ANGULAR_BINS)
    reluct_cell, eddy_cell, loss_cell = lookup(regions, (inverse_permeability, electric_conductance, core_dissipation_coefficient))
    plane_cell, axial_cell, local_thermal_storage = lookup(regions, (inplane_thermal_conductance, through_plane_conductance, thermal_storage))
    stacked = jnp.concatenate([magnetic_vector_field, reluct_cell[None]], axis=0)
    curl_term, flux = em_terms(pad_grid(stacked))
    magnetic_misfit = curl_term + eddy_cell * magnetic_vector_field - imposed_current_density
    thermal_rhs = loss_cell * jnp.sum(flux * flux, axis=0)
    right_hand_sides = jnp.stack([local_thermal_storage * prior_thermal_state + thermal_rhs, goal_sensitivity])
    repeat_relaxation_passes = jnp.stack([prior_thermal_state, jnp.zeros_like(prior_thermal_state)])
    for iteration in range(SWEEPS):
        combined = jnp.concatenate([repeat_relaxation_passes, plane_cell[None], axial_cell[None]], axis=0)
        padded = jnp.pad(combined, ((0, 0), (0, 0), (1, 1), (1, 1)))
        repeat_relaxation_passes = relax(padded, local_thermal_storage, right_hand_sides)
    thermal_state = repeat_relaxation_passes[0]
    dual_magnetic_rhs = 2.0 * loss_cell * repeat_relaxation_passes[1] * flux
    return magnetic_misfit, dual_magnetic_rhs, thermal_state
```

```python
import functools
import jax
import jax.numpy as jnp
from jax import lax
from jax.experimental import pallas as pl
from jax.experimental.pallas import tpu as pltpu
from jax.sharding import PartitionSpec as P

NREG = 8
SWEEPS = 4
NA = 32
F32 = jnp.float32
VM = pl.BlockSpec(memory_space=pltpu.VMEM)
SM = pl.BlockSpec(memory_space=pltpu.SMEM)


def params(mib):
    return pltpu.CompilerParams(vmem_limit_bytes=mib * 1024 * 1024)


def sub_low(shape):
    return lax.broadcasted_iota(jnp.int32, shape, len(shape) - 2) % 8 < 4


def pack_down(first, second):
    return jnp.where(sub_low(first.shape), first, pltpu.roll(second, 4, 0))


def pack_up(first, second):
    return jnp.where(sub_low(first.shape), pltpu.roll(first, 4, 0), second)


def unpack_first(from_next, from_prev):
    return jnp.where(sub_low(from_next.shape), from_next, pltpu.roll(from_prev, 4, 0))


def unpack_second(from_next, from_prev):
    return jnp.where(sub_low(from_next.shape), pltpu.roll(from_next, 4, 0), from_prev)


def lookup(region, tables):
    found = [jnp.zeros(region.shape, F32) for _ in tables]
    for k in range(NREG):
        match = region == float(k + 1)
        found = [jnp.where(match, t[k], f) for t, f in zip(tables, found)]
    return found


def send_kernel(pot, fixed, spin, offs, prior, goal, out, region_out, prior_down, prior_up):
    section = lax.axis_index("section")
    azim = lax.axis_index("azim")
    shifted = (azim - offs[...]) & (NA - 1)
    rows = lax.broadcasted_iota(jnp.int32, (NA, 128), 0)
    hot = jnp.where(rows == shifted, 1.0, 0.0).astype(jnp.bfloat16)
    rotor = lax.dot_general(
        spin[...].astype(F32).astype(jnp.bfloat16), hot, (((0,), (0,)), ((), ())), preferred_element_type=F32
    )
    stator = fixed[0].astype(F32)
    inner = jnp.where(section == 0, rotor, stator[:128])
    region_out[:128] = inner + 1.0
    region_out[128:] = stator[128:] + 1.0
    for j in range(NA):
        at = pl.ds(8 * j, 8)
        for f in range(3):
            out[j, pl.ds(8 * f, 8), :] = pot[f, 0, at, :]
        out[j, pl.ds(24, 8), :] = region_out[at, :]
        prior_down[j] = pack_down(prior[j], goal[j])
        prior_up[j] = pack_up(prior[j], goal[j])


def rows_kernel(got, down, up):
    for a in range(NA):
        for p in range(2):
            first = got[a, pl.ds(16 * p, 8), :]
            second = got[a, pl.ds(16 * p + 8, 8), :]
            down[a, pl.ds(8 * p, 8), :] = pack_down(first, second)
            up[a, pl.ds(8 * p, 8), :] = pack_up(first, second)


def window(got, prior, goal, from_next, from_prev, heat_next, heat_prev, a):
    tiles = []
    for p in range(2):
        nxt = from_next[a, pl.ds(8 * p, 8), :]
        prv = from_prev[a, pl.ds(8 * p, 8), :]
        tiles.append((got[a, pl.ds(16 * p, 8), :], unpack_first(nxt, prv)))
        tiles.append((got[a, pl.ds(16 * p + 8, 8), :], unpack_second(nxt, prv)))
    nxt, prv = heat_next[a], heat_prev[a]
    tiles.append((prior[a], unpack_first(nxt, prv)))
    tiles.append((goal[a], unpack_second(nxt, prv)))
    return tiles


def layers_kernel(got, prior, goal, from_next, from_prev, heat_next, heat_prev, edge):
    lane = lax.broadcasted_iota(jnp.int32, (8, 128), 1) // 8

    def step(a, carry):
        tiles = window(got, prior, goal, from_next, from_prev, heat_next, heat_prev, a)
        packed = jnp.zeros((8, 128), F32)
        for f in range(6):
            for t in range(2):
                c = 2 * f + t
                packed = jnp.where(lane == c, pltpu.roll(tiles[f][t], 4 + 8 * c, 1), packed)
        edge[a] = packed
        return carry

    lax.fori_loop(0, NA, step, 0)


def rnext(v):
    return pltpu.roll(v, 15, 0)


def rprev(v):
    return pltpu.roll(v, 1, 0)


def lnext(v):
    return pltpu.roll(v, 255, 1)


def lprev(v):
    return pltpu.roll(v, 1, 1)


def heat_kernel(
    got, prior, goal, from_next, from_prev, heat_next, heat_prev, edge_core, edge_far,
    reluct, loss, plane, axial, storage, out,
    pot, mats, pri, sens, coef, base, flux, hfield, temp, adj,
):
    odd = lax.axis_index("axial") % 2 == 1
    lane = lax.broadcasted_iota(jnp.int32, (8, 128), 1)
    from_right = lane % 8 >= 4
    near = (lane < 4) | (lane >= 124)

    def gather(a, carry):
        tiles = window(got, prior, goal, from_next, from_prev, heat_next, heat_prev, a)
        core, far = edge_core[a], edge_far[a]
        pick_core = from_right != odd
        merged = jnp.where(pick_core, core, far)
        wide = []
        for f in range(6):
            ends = []
            for t in range(2):
                c = 2 * f + t
                ends.append(jnp.where(near, pltpu.roll(merged, 124 - 8 * c, 1), 0.0))
            main = jnp.concatenate([tiles[f][0], tiles[f][1]], axis=0)
            side = jnp.concatenate([ends[0], ends[1]], axis=0)
            wide.append(jnp.concatenate([main, side], axis=1))
        for f in range(3):
            pot[f, a] = wide[f]
        found = lookup(wide[3], (reluct, loss, plane, axial, storage))
        for m in range(5):
            mats[m, a] = found[m]
        pri[a] = wide[4]
        sens[a] = wide[5]
        return carry

    lax.fori_loop(0, NA, gather, 0)

    def prepare(a, carry):
        up = (a + 1) & (NA - 1)
        down = (a - 1) & (NA - 1)
        pa, pr, pz = pot[0, a], pot[1, a], pot[2, a]
        fa = (rnext(pz) - pz) - (lnext(pr) - pr)
        fr = (lnext(pa) - pa) - (pot[2, up] - pz)
        fz = (pot[1, up] - pr) - (rnext(pa) - pa)
        flux[0, a] = fa[:8, :128]
        flux[1, a] = fr[:8, :128]
        flux[2, a] = fz[:8, :128]
        rel, dens, kp, ka, cap = (mats[m, a] for m in range(5))
        hfield[0, a] = rel * fa
        hfield[1, a] = rel * fr
        hfield[2, a] = rel * fz
        source = cap * pri[a] + dens * (fa * fa + fr * fr + fz * fz)
        w = [
            0.5 * (kp + mats[2, up]), 0.5 * (kp + mats[2, down]),
            0.5 * (kp + rnext(kp)), 0.5 * (kp + rprev(kp)),
            0.5 * (ka + lnext(ka)), 0.5 * (ka + lprev(ka)),
        ]
        total = cap + (((((w[0] + w[1]) + w[2]) + w[3]) + w[4]) + w[5])
        inside = cap > 0.0
        inv = jnp.where(inside, 1.0 / jnp.where(inside, total, 1.0), 0.0)
        for n in range(6):
            coef[n, a] = inv * w[n]
        base[0, a] = inv * source
        first = inv * sens[a]
        base[1, a] = first
        adj[0, a] = first
        return carry

    lax.fori_loop(0, NA, prepare, 0)

    def relax(field, slot, a, c, b):
        up = (a + 1) & (NA - 1)
        down = (a - 1) & (NA - 1)
        v = field(a)
        total = b + c[0] * field(up) + c[1] * field(down)
        total = total + c[2] * rnext(v) + c[3] * rprev(v)
        return total + c[4] * lnext(v) + c[5] * lprev(v)

    for sweep in range(SWEEPS):
        now, later = sweep % 2, (sweep + 1) % 2

        def step(a, carry, sweep=sweep, now=now, later=later):
            c = [coef[n, a] for n in range(6)]
            if sweep == 0:
                temp[later, a] = relax(lambda i: pri[i], later, a, c, base[0, a])
            else:
                temp[later, a] = relax(lambda i: temp[now, i], later, a, c, base[0, a])
                adj[now, a] = relax(lambda i: adj[later, i], later, a, c, base[1, a])
            return carry

        lax.fori_loop(0, NA, step, 0)

    last_t = SWEEPS % 2
    last_a = (SWEEPS - 1) % 2

    def finish(a, carry):
        down = (a - 1) & (NA - 1)
        scale = 2.0 * mats[1, a][:8, :128] * adj[last_a, a][:8, :128]
        ha, hr, hz = hfield[0, a], hfield[1, a], hfield[2, a]
        ca = (lprev(hr) - hr) - (rprev(hz) - hz)
        cr = (hfield[2, down] - hz) - (lprev(ha) - ha)
        cz = (rprev(ha) - ha) - (hfield[1, down] - hr)
        out[a, pl.ds(0, 8), :] = ca[:8, :128]
        out[a, pl.ds(8, 8), :] = cr[:8, :128]
        out[a, pl.ds(16, 8), :] = cz[:8, :128]
        for f in range(3):
            out[a, pl.ds(24 + 8 * f, 8), :] = scale * flux[f, a]
        out[a, pl.ds(48, 8), :] = temp[last_t, a][:8, :128]
        return carry

    lax.fori_loop(0, NA, finish, 0)


def finish_kernel(got, region, pot, current, eddy, misfit, dual, state):
    def step(j, carry):
        at = pl.ds(pl.multiple_of(8 * j, 8), 8)
        (sigma,) = lookup(region[at, :], (eddy,))
        for f in range(3):
            curl = got[j, pl.ds(8 * f, 8), :]
            misfit[f, 0, at, :] = curl + sigma * pot[f, 0, at, :] - current[f, 0, at, :]
            dual[f, 0, at, :] = got[j, pl.ds(24 + 8 * f, 8), :]
        state[0, at, :] = got[j, pl.ds(48, 8), :]
        return carry

    lax.fori_loop(0, NA, step, 0)


def struct(*shape):
    return jax.ShapeDtypeStruct(shape, F32)


def body(
    magnetic_vector_field,
    imposed_current_density,
    fixed_material_map,
    spinning_material_map,
    slab_slide_offsets,
    inverse_permeability,
    electric_conductance,
    core_dissipation_coefficient,
    inplane_thermal_conductance,
    through_plane_conductance,
    thermal_storage,
    prior_thermal_state,
    goal_sensitivity,
):
    rows = lax.axis_size("section") * lax.axis_size("azim")
    chain = ("section", "azim")
    onward = [(i, i + 1) for i in range(rows - 1)]
    backward = [(i + 1, i) for i in range(rows - 1)]
    cores = [(0, 1), (1, 0), (2, 3), (3, 2)]
    far = [(1, 2), (2, 1)]

    payload, region, heat_down, heat_up = pl.pallas_call(
        send_kernel,
        out_shape=(struct(NA, 32, 128), struct(256, 128), struct(NA, 8, 128), struct(NA, 8, 128)),
        in_specs=[VM] * 6,
        out_specs=(VM,) * 4,
        compiler_params=params(16),
        name="send",
    )(
        magnetic_vector_field, fixed_material_map, spinning_material_map,
        slab_slide_offsets.reshape(1, 128), prior_thermal_state, goal_sensitivity,
    )
    heat_prev = lax.ppermute(heat_up, chain, onward)
    heat_next = lax.ppermute(heat_down, chain, backward)
    got = lax.all_to_all(payload, "azim", split_axis=0, concat_axis=0, tiled=True)
    down, up = pl.pallas_call(
        rows_kernel,
        out_shape=(struct(NA, 16, 128), struct(NA, 16, 128)),
        in_specs=[VM],
        out_specs=(VM, VM),
        compiler_params=params(8),
        name="pack_rows",
    )(got)
    from_prev = lax.ppermute(up, chain, onward)
    from_next = lax.ppermute(down, chain, backward)
    heat_args = (got, prior_thermal_state, goal_sensitivity, from_next, from_prev, heat_next, heat_prev)
    edge = pl.pallas_call(
        layers_kernel,
        out_shape=struct(NA, 8, 128),
        in_specs=[VM] * 7,
        out_specs=VM,
        compiler_params=params(8),
        name="pack_layers",
    )(*heat_args)
    edge_core = lax.ppermute(edge, "axial", cores)
    edge_far = lax.ppermute(edge, "axial", far)
    wide = (NA, 16, 256)
    result = pl.pallas_call(
        heat_kernel,
        out_shape=struct(NA, 56, 128),
        in_specs=[VM] * 9 + [SM] * 5,
        out_specs=VM,
        scratch_shapes=[
            pltpu.VMEM((3,) + wide, F32),
            pltpu.VMEM((5,) + wide, F32),
            pltpu.VMEM(wide, F32),
            pltpu.VMEM(wide, F32),
            pltpu.VMEM((6,) + wide, F32),
            pltpu.VMEM((2,) + wide, F32),
            pltpu.VMEM((3, NA, 8, 128), F32),
            pltpu.VMEM((3,) + wide, F32),
            pltpu.VMEM((2,) + wide, F32),
            pltpu.VMEM((2,) + wide, F32),
        ],
        compiler_params=params(32),
        name="heat",
    )(
        *heat_args, edge_core, edge_far,
        inverse_permeability, core_dissipation_coefficient, inplane_thermal_conductance,
        through_plane_conductance, thermal_storage,
    )
    back = lax.all_to_all(result, "azim", split_axis=0, concat_axis=0, tiled=True)
    return pl.pallas_call(
        finish_kernel,
        out_shape=(struct(3, 1, 256, 128), struct(3, 1, 256, 128), struct(1, 256, 128)),
        in_specs=[VM] * 4 + [SM],
        out_specs=(VM,) * 3,
        compiler_params=params(16),
        name="finish",
    )(back, region, magnetic_vector_field, imposed_current_density, electric_conductance)


def solution(mesh):
    in_specs = (
        P(None, "azim", "section", "axial"),
        P(None, "azim", "section", "axial"),
        P("azim", "section", "axial"),
        P(),
        P("axial"),
        P(),
        P(),
        P(),
        P(),
        P(),
        P(),
        P(None, ("section", "azim"), "axial"),
        P(None, ("section", "azim"), "axial"),
    )
    out_specs = (
        P(None, "azim", "section", "axial"),
        P(None, "azim", "section", "axial"),
        P("azim", "section", "axial"),
    )
    return jax.shard_map(body, mesh=mesh, in_specs=in_specs, out_specs=out_specs, check_vma=False)
```

```python
import jax
import jax.numpy as jnp
from jax import lax
from jax.experimental import pallas as pl
from jax.experimental.pallas import tpu as pltpu
from jax.sharding import PartitionSpec as P

NREG = 8
SWEEPS = 4
NA = 32
F32 = jnp.float32
VM = pl.BlockSpec(memory_space=pltpu.VMEM)
SM = pl.BlockSpec(memory_space=pltpu.SMEM)
HBM = pl.BlockSpec(memory_space=pl.ANY)


def params(mib):
    return pltpu.CompilerParams(vmem_limit_bytes=mib * 1024 * 1024)


def struct(*shape):
    return jax.ShapeDtypeStruct(shape, F32)


def sub_low():
    return lax.broadcasted_iota(jnp.int32, (8, 128), 0) < 4


def lanes():
    return lax.broadcasted_iota(jnp.int32, (8, 128), 1)


def put(packed, slot, tile):
    return jnp.where(lanes() // 8 == slot, pltpu.roll(tile, 4 + 8 * slot, 1), packed)


def take(packed, slot):
    lane = lanes()
    return jnp.where((lane < 4) | (lane >= 124), pltpu.roll(packed, 124 - 8 * slot, 1), 0.0)


def lookup(region, tables):
    found = [jnp.zeros(region.shape, F32) for _ in tables]
    for k in range(NREG):
        match = region == float(k + 1)
        found = [jnp.where(match, t[k], f) for t, f in zip(tables, found)]
    return found


def send_kernel(
    pot_in, fixed_in, spin_in, offs_in, prior_in, goal_in,
    region, frame, ring, heat_down, heat_up,
    pot, fixed, spin, offs, prior, goal, sems,
):
    pairs = ((pot_in, pot), (fixed_in, fixed), (spin_in, spin), (offs_in, offs), (prior_in, prior), (goal_in, goal))
    copies = [pltpu.make_async_copy(src, dst, sems.at[n]) for n, (src, dst) in enumerate(pairs)]
    for copy in copies:
        copy.start()
    for copy in copies[1:4]:
        copy.wait()
    section = lax.axis_index("section")
    azim = lax.axis_index("azim")
    shifted = (azim - offs[...]) & (NA - 1)
    rows = lax.broadcasted_iota(jnp.int32, (NA, 128), 0)
    hot = jnp.where(rows == shifted, 1.0, 0.0).astype(jnp.bfloat16)
    rotor = lax.dot_general(
        spin[...].astype(F32).astype(jnp.bfloat16), hot, (((0,), (0,)), ((), ())), preferred_element_type=F32
    )
    stator = fixed[0].astype(F32)
    region[:128] = jnp.where(section == 0, rotor, stator[:128]) + 1.0
    region[128:] = stator[128:] + 1.0
    copies[0].wait()
    low = sub_low()

    def tile(f, t):
        at = pl.ds(8 * t, 8)
        return region[at, :] if f == 3 else pot[f, 0, at, :]

    for f in range(4):
        frame[pl.ds(8 * f, 8), :] = jnp.where(low, tile(f, 0), tile(f, 31))
    for g in range(8):
        packed = jnp.zeros((8, 128), F32)
        for u in range(4):
            for f in range(4):
                packed = put(packed, 4 * u + f, tile(f, 4 * g + u))
        frame[pl.ds(32 + 8 * g, 8), :] = packed
    ring[0] = pot[1, 0]
    ring[1] = pot[2, 0]
    copies[4].wait()
    copies[5].wait()
    for a in range(NA):
        heat_down[a] = jnp.where(low, prior[a], pltpu.roll(goal[a], 4, 0))
        heat_up[a] = jnp.where(low, pltpu.roll(prior[a], 4, 0), goal[a])


def beside(gathered, own, step, count, at):
    index = own + step
    valid = (index >= 0) & (index < count)
    safe = jnp.clip(index, 0, count - 1)
    return jnp.where(valid, gathered[at(safe)], 0.0)


def halo_kernel(frames, halo):
    section = lax.axis_index("section")
    axial = lax.axis_index("axial")
    other = 1 - section
    lane = lanes()
    right = lane % 8 >= 4
    valid = sub_low() == (section == 0)
    for g in range(8):
        at = pl.ds(32 + 8 * g, 8)
        after = beside(frames, axial, 1, 4, lambda b: (4 * section + b, at, slice(None)))
        before = beside(frames, axial, -1, 4, lambda b: (4 * section + b, at, slice(None)))
        halo[g] = jnp.where(right, after, before)
    for f in range(4):
        at = pl.ds(8 * f, 8)
        halo[8 + f] = jnp.where(valid, frames[4 * other + axial, at, :], 0.0)
        after = beside(frames, axial, 1, 4, lambda b: (4 * other + b, at, slice(None)))
        before = beside(frames, axial, -1, 4, lambda b: (4 * other + b, at, slice(None)))
        ends = jnp.where(lane < 4, after, jnp.where(lane >= 124, before, 0.0))
        halo[12 + f] = jnp.where(valid, ends, 0.0)


def heat_tiles(prior, goal, from_next, from_prev, a):
    low = sub_low()
    nxt, prv = from_next[a], from_prev[a]
    return (
        (prior[a], jnp.where(low, nxt, pltpu.roll(prv, 4, 0))),
        (goal[a], jnp.where(low, pltpu.roll(nxt, 4, 0), prv)),
    )


def layers_kernel(prior, goal, from_next, from_prev, edge):
    for g in range(NA // 4):
        packed = jnp.zeros((8, 128), F32)
        for u in range(4):
            tiles = heat_tiles(prior, goal, from_next, from_prev, 4 * g + u)
            for f in range(2):
                for t in range(2):
                    packed = put(packed, 4 * u + 2 * f + t, tiles[f][t])
        edge[g] = packed


def rnext(v):
    return pltpu.roll(v, 15, 0)


def rprev(v):
    return pltpu.roll(v, 1, 0)


def lnext(v):
    return pltpu.roll(v, 255, 1)


def lprev(v):
    return pltpu.roll(v, 1, 1)


def magnetic_kernel(
    pot, region, halo, ring, ring_halo, current, reluct, eddy, loss,
    payload, misfit, weight, hring,
    wide, heat, hfield,
):
    low = sub_low()
    mains = [
        lambda at: pot[0, 0, at, :], lambda at: pot[1, 0, at, :], lambda at: pot[2, 0, at, :],
        lambda at: region[at, :], lambda at: ring[0, at, :], lambda at: ring[1, at, :],
    ]
    left, right = pl.ds(0, 128), pl.ds(128, 128)
    for n in range(6):
        source, f = (halo, n) if n < 4 else (ring_halo, n - 3)
        for t in range(32):
            wide[n, pl.ds(8 + 8 * t, 8), left] = mains[n](pl.ds(8 * t, 8))
            wide[n, pl.ds(8 + 8 * t, 8), right] = take(source[t // 4], 4 * (t % 4) + f)
        for side, block in ((left, source[8 + f]), (right, source[12 + f])):
            wide[n, pl.ds(264, 8), side] = jnp.where(low, block, 0.0)
            wide[n, pl.ds(0, 8), side] = jnp.where(low, 0.0, block)
            wide[n, pl.ds(272, 8), side] = jnp.zeros((8, 128), F32)
    for t in range(34):
        here, ahead = pl.ds(8 * t, 8), pl.ds(8 * t + 1, 8)
        pa, pr, pz = wide[0, here, :], wide[1, here, :], wide[2, here, :]
        fa = (wide[2, ahead, :] - pz) - (lnext(pr) - pr)
        fr = (lnext(pa) - pa) - (wide[5, here, :] - pz)
        fz = (wide[4, here, :] - pr) - (wide[0, ahead, :] - pa)
        rel, dens = lookup(wide[3, here, :], (reluct, loss))
        heat[t] = dens * (fa * fa + fr * fr + fz * fz)
        hfield[0, here, :] = rel * fa
        hfield[1, here, :] = rel * fr
        hfield[2, here, :] = rel * fz
        if 1 <= t <= 32:
            rows = pl.ds(8 * t - 8, 8)
            scale = 2.0 * dens
            for n, f in enumerate((fa, fr, fz)):
                weight[n, rows, :] = (scale * f)[:, :128]
            hring[0, rows, :] = (rel * fr)[:, :128]
            hring[1, rows, :] = (rel * fz)[:, :128]
    for t in range(1, 33):
        here, behind, rows = pl.ds(8 * t, 8), pl.ds(8 * t - 1, 8), pl.ds(8 * t - 8, 8)
        ha, hr, hz = hfield[0, here, :], hfield[1, here, :], hfield[2, here, :]
        ca = (lprev(hr) - hr) - (hfield[2, behind, :] - hz)
        cr = -hz - (lprev(ha) - ha)
        cz = (hfield[0, behind, :] - ha) + hr
        (sigma,) = lookup(region[rows, :], (eddy,))
        for n, c in enumerate((ca, cr, cz)):
            misfit[n, rows, :] = c[:, :128] + (sigma * pot[n, 0, rows, :] - current[n, 0, rows, :])
    for j in range(NA):
        t = j + 1
        packed = jnp.zeros((8, 128), F32)
        tiles = []
        for get in (lambda i: heat[i], lambda i: wide[3, pl.ds(8 * i, 8), :]):
            near, after, before = get(t), get(t + 1), get(t - 1)
            beyond = [jnp.where(low, after[:, k:k + 128], before[:, k:k + 128]) for k in (0, 128)]
            tiles.append((near[:, :128], near[:, 128:]))
            tiles.append(tuple(beyond))
        for c, (main, side) in enumerate(tiles):
            payload[j, pl.ds(8 * c, 8), :] = main
            packed = put(packed, c, side)
        payload[j, pl.ds(32, 8), :] = packed


def heat_kernel(
    got, prior, goal, from_next, from_prev, edges,
    plane, axial, storage, out,
    kin, kax, cap, pri, sens, src, coef, base, temp0, temp1, adj0, adj1,
):
    own = lax.axis_index("axial")
    right = lanes() % 8 >= 4

    def join(tiles, ends):
        return jnp.concatenate([jnp.concatenate(tiles, axis=0), jnp.concatenate(ends, axis=0)], axis=1)

    def gather(g, carry):
        after = beside(edges, own, 1, 4, lambda b: (b, g))
        before = beside(edges, own, -1, 4, lambda b: (b, g))
        merged = jnp.where(right, after, before)
        for u in range(4):
            a = 4 * g + u
            side = got[a, pl.ds(32, 8), :]
            tiles = [got[a, pl.ds(8 * c, 8), :] for c in range(4)]
            ends = [take(side, c) for c in range(4)]
            src[a] = join(tiles[:2], ends[:2])
            kin[a], kax[a], cap[a] = lookup(join(tiles[2:], ends[2:]), (plane, axial, storage))
            held = heat_tiles(prior, goal, from_next, from_prev, a)
            pri[a] = join(held[0], [take(merged, 4 * u + t) for t in range(2)])
            sens[a] = join(held[1], [take(merged, 4 * u + 2 + t) for t in range(2)])
        return carry

    lax.fori_loop(0, NA // 4, gather, 0, unroll=2)

    def prepare(a, carry):
        up = (a + 1) & (NA - 1)
        down = (a - 1) & (NA - 1)
        kp, ka, c = kin[a], kax[a], cap[a]
        source = c * pri[a] + src[a]
        w = [
            0.5 * (kp + kin[up]), 0.5 * (kp + kin[down]),
            0.5 * (kp + rnext(kp)), 0.5 * (kp + rprev(kp)),
            0.5 * (ka + lnext(ka)), 0.5 * (ka + lprev(ka)),
        ]
        total = c + (((((w[0] + w[1]) + w[2]) + w[3]) + w[4]) + w[5])
        inside = c > 0.0
        inv = jnp.where(inside, 1.0 / jnp.where(inside, total, 1.0), 0.0)
        for n in range(6):
            coef[n, a] = inv * w[n]
        base[0, a] = inv * source
        first = inv * sens[a]
        base[1, a] = first
        adj0[a] = first
        return carry

    lax.fori_loop(0, NA, prepare, 0, unroll=8)

    def relax(field, a, c, b):
        up = (a + 1) & (NA - 1)
        down = (a - 1) & (NA - 1)
        v = field[a]
        total = b + c[0] * field[up] + c[1] * field[down]
        total = total + c[2] * rnext(v) + c[3] * rprev(v)
        return total + c[4] * lnext(v) + c[5] * lprev(v)

    temps = [pri, temp0, temp1, temp0, temp1]
    adjs = [None, adj0, adj1, adj0, adj1]
    for sweep in range(SWEEPS):

        def step(a, carry, sweep=sweep):
            c = [coef[n, a] for n in range(6)]
            t = relax(temps[sweep], a, c, base[0, a])
            if sweep == SWEEPS - 1:
                out[a, pl.ds(0, 8), :] = t[:8, :128]
            else:
                temps[sweep + 1][a] = t
            if sweep > 0:
                s = relax(adjs[sweep], a, c, base[1, a])
                if sweep == SWEEPS - 1:
                    out[a, pl.ds(8, 8), :] = s[:8, :128]
                else:
                    adjs[sweep + 1][a] = s
            return carry

        lax.fori_loop(0, NA, step, 0, unroll=8)


def finish_kernel(got, part, weight, hring, misfit, dual, state):
    misfit[0, 0] = part[0]
    misfit[1, 0] = part[1] + hring[1]
    misfit[2, 0] = part[2] - hring[0]

    def step(j, carry):
        at = pl.ds(pl.multiple_of(8 * j, 8), 8)
        state[0, at, :] = got[j, pl.ds(0, 8), :]
        adjoint = got[j, pl.ds(8, 8), :]
        for f in range(3):
            dual[f, 0, at, :] = weight[f, at, :] * adjoint
        return carry

    lax.fori_loop(0, NA, step, 0, unroll=8)


def body(
    magnetic_vector_field,
    imposed_current_density,
    fixed_material_map,
    spinning_material_map,
    slab_slide_offsets,
    inverse_permeability,
    electric_conductance,
    core_dissipation_coefficient,
    inplane_thermal_conductance,
    through_plane_conductance,
    thermal_storage,
    prior_thermal_state,
    goal_sensitivity,
):
    rows = lax.axis_size("section") * lax.axis_size("azim")
    chain = ("section", "azim")
    onward = [(i, i + 1) for i in range(rows - 1)]
    backward = [(i + 1, i) for i in range(rows - 1)]
    from_after = [((i + 1) % NA, i) for i in range(NA)]
    from_before = [(i, (i + 1) % NA) for i in range(NA)]

    region, frame, ring, heat_down, heat_up = pl.pallas_call(
        send_kernel,
        out_shape=(
            struct(256, 128), struct(96, 128), struct(2, 256, 128), struct(NA, 8, 128), struct(NA, 8, 128),
        ),
        in_specs=[HBM] * 6,
        out_specs=(VM,) * 5,
        scratch_shapes=[
            pltpu.VMEM((3, 1, 256, 128), F32),
            pltpu.VMEM((1, 256, 128), jnp.int32),
            pltpu.VMEM((NA, 128), jnp.int32),
            pltpu.VMEM((1, 128), jnp.int32),
            pltpu.VMEM((NA, 8, 128), F32),
            pltpu.VMEM((NA, 8, 128), F32),
            pltpu.SemaphoreType.DMA((6,)),
        ],
        compiler_params=params(62),
        name="send",
    )(
        magnetic_vector_field, fixed_material_map, spinning_material_map,
        slab_slide_offsets.reshape(1, 128), prior_thermal_state, goal_sensitivity,
    )
    frames = lax.all_gather(frame, ("section", "axial"))
    ring_main = lax.ppermute(ring, "azim", from_after)
    heat_prev = lax.ppermute(heat_up, chain, onward)
    heat_next = lax.ppermute(heat_down, chain, backward)
    halo = pl.pallas_call(
        halo_kernel, out_shape=struct(16, 8, 128), in_specs=[VM], out_specs=VM,
        compiler_params=params(8), name="halo",
    )(frames)
    ring_halo = lax.ppermute(halo, "azim", from_after)
    heat_args = (prior_thermal_state, goal_sensitivity, heat_next, heat_prev)
    edge = pl.pallas_call(
        layers_kernel, out_shape=struct(8, 8, 128), in_specs=[VM] * 4, out_specs=VM,
        compiler_params=params(8), name="layers",
    )(*heat_args)
    edges = lax.all_gather(edge, "axial")
    payload, part, weight, hring = pl.pallas_call(
        magnetic_kernel,
        out_shape=(struct(NA, 40, 128), struct(3, 256, 128), struct(3, 256, 128), struct(2, 256, 128)),
        in_specs=[VM] * 6 + [SM] * 3,
        out_specs=(VM,) * 4,
        scratch_shapes=[
            pltpu.VMEM((6, 280, 256), F32),
            pltpu.VMEM((34, 8, 256), F32),
            pltpu.VMEM((3, 272, 256), F32),
        ],
        compiler_params=params(24),
        name="magnetic",
    )(
        magnetic_vector_field, region, halo, ring_main, ring_halo, imposed_current_density,
        inverse_permeability, electric_conductance, core_dissipation_coefficient,
    )
    got = lax.all_to_all(payload, "azim", split_axis=0, concat_axis=0, tiled=True)
    hring = lax.ppermute(hring, "azim", from_before)
    wide = pltpu.VMEM((NA, 16, 256), F32)
    result = pl.pallas_call(
        heat_kernel,
        out_shape=struct(NA, 16, 128),
        in_specs=[VM] * 6 + [SM] * 3,
        out_specs=VM,
        scratch_shapes=[
            wide, wide, wide, wide, wide, wide,
            pltpu.VMEM((6, NA, 16, 256), F32),
            pltpu.VMEM((2, NA, 16, 256), F32),
            wide, wide, wide, wide,
        ],
        compiler_params=params(32),
        name="heat",
    )(
        got, *heat_args, edges,
        inplane_thermal_conductance, through_plane_conductance, thermal_storage,
    )
    back = lax.all_to_all(result, "azim", split_axis=0, concat_axis=0, tiled=True)
    return pl.pallas_call(
        finish_kernel,
        out_shape=(struct(3, 1, 256, 128), struct(3, 1, 256, 128), struct(1, 256, 128)),
        in_specs=[VM] * 4,
        out_specs=(VM,) * 3,
        compiler_params=params(16),
        name="finish",
    )(back, part, weight, hring)


def solution(mesh):
    in_specs = (
        P(None, "azim", "section", "axial"),
        P(None, "azim", "section", "axial"),
        P("azim", "section", "axial"),
        P(),
        P("axial"),
        P(),
        P(),
        P(),
        P(),
        P(),
        P(),
        P(None, ("section", "azim"), "axial"),
        P(None, ("section", "azim"), "axial"),
    )
    out_specs = (
        P(None, "azim", "section", "axial"),
        P(None, "azim", "section", "axial"),
        P("azim", "section", "axial"),
    )
    return jax.shard_map(body, mesh=mesh, in_specs=in_specs, out_specs=out_specs, check_vma=False)
```

```python
import jax
import jax.numpy as jnp
from jax import lax
from jax.experimental import pallas as pl
from jax.experimental.pallas import tpu as pltpu
from jax.sharding import PartitionSpec as P

NREG = 8
SWEEPS = 4
NA = 32
F32 = jnp.float32
VM = pl.BlockSpec(memory_space=pltpu.VMEM)
SM = pl.BlockSpec(memory_space=pltpu.SMEM)
HBM = pl.BlockSpec(memory_space=pl.ANY)


def params(mib):
    return pltpu.CompilerParams(vmem_limit_bytes=mib * 1024 * 1024)


def struct(*shape):
    return jax.ShapeDtypeStruct(shape, F32)


def sub_low():
    return lax.broadcasted_iota(jnp.int32, (8, 128), 0) < 4


def lanes():
    return lax.broadcasted_iota(jnp.int32, (8, 128), 1)


def put(packed, slot, tile):
    return jnp.where(lanes() // 8 == slot, pltpu.roll(tile, 4 + 8 * slot, 1), packed)


def take(packed, slot):
    lane = lanes()
    return jnp.where((lane < 4) | (lane >= 124), pltpu.roll(packed, 124 - 8 * slot, 1), 0.0)


def lookup(region, tables):
    found = [jnp.zeros(region.shape, F32) for _ in tables]
    for k in range(NREG):
        match = region == float(k + 1)
        found = [jnp.where(match, t[k], f) for t, f in zip(tables, found)]
    return found


def find_region(fixed, spin, offs, region):
    section = lax.axis_index("section")
    azim = lax.axis_index("azim")
    shifted = (azim - offs[...]) & (NA - 1)
    rows = lax.broadcasted_iota(jnp.int32, (NA, 128), 0)
    hot = jnp.where(rows == shifted, 1.0, 0.0).astype(jnp.bfloat16)
    rotor = lax.dot_general(
        spin[...].astype(F32).astype(jnp.bfloat16), hot, (((0,), (0,)), ((), ())), preferred_element_type=F32
    )
    stator = fixed[0].astype(F32)
    region[:128] = jnp.where(section == 0, rotor, stator[:128]) + 1.0
    region[128:] = stator[128:] + 1.0


def send_kernel(
    pot_in, fixed_in, spin_in, offs_in, prior_in, goal_in,
    row_edge, frame, ring,
    pot, fixed, spin, offs, prior, goal, region, sems,
):
    pairs = ((pot_in, pot), (fixed_in, fixed), (spin_in, spin), (offs_in, offs), (prior_in, prior), (goal_in, goal))
    copies = [pltpu.make_async_copy(src, dst, sems.at[n]) for n, (src, dst) in enumerate(pairs)]
    for copy in copies:
        copy.start()
    for copy in copies[1:4]:
        copy.wait()
    find_region(fixed, spin, offs, region)
    copies[0].wait()
    low = sub_low()

    def tile(f, t):
        at = pl.ds(8 * t, 8)
        return region[at, :] if f == 3 else pot[f, 0, at, :]

    for f in range(4):
        row_edge[f] = jnp.where(low, tile(f, 0), tile(f, 31))
    for g in range(8):
        packed = jnp.zeros((8, 128), F32)
        for u in range(4):
            for f in range(4):
                packed = put(packed, 4 * u + f, tile(f, 4 * g + u))
        frame[g] = packed
    ring[0] = pot[1, 0]
    ring[1] = pot[2, 0]
    copies[4].wait()
    copies[5].wait()
    for g in range(4):
        packed = jnp.zeros((8, 128), F32)
        for u in range(8):
            packed = put(packed, 2 * u, prior[8 * g + u])
            packed = put(packed, 2 * u + 1, goal[8 * g + u])
        frame[8 + g] = packed


def frame_kernel(frame, across, out):
    valid = sub_low() == (lax.axis_index("section") == 0)
    for g in range(12):
        out[g] = frame[g]
    for f in range(4):
        out[12 + f] = jnp.where(valid, across[f], 0.0)


def halo_kernel(own, core, far, prior, goal, halo, heat_down, heat_up):
    odd = lax.axis_index("axial") % 2 == 1
    lane = lanes()
    low = sub_low()
    right = lane % 8 >= 4
    for g in range(16):
        after = jnp.where(odd, far[g], core[g])
        before = jnp.where(odd, core[g], far[g])
        if g < 8:
            halo[g] = jnp.where(right, after, before)
        elif g < 12:
            merged = jnp.where(right, after, before)
            heat_down[24 + g] = merged
            heat_up[24 + g] = merged
        else:
            halo[g - 4] = own[g]
            halo[g] = jnp.where(lane < 4, after, jnp.where(lane >= 124, before, 0.0))
    for a in range(NA):
        heat_down[a] = jnp.where(low, prior[a], pltpu.roll(goal[a], 4, 0))
        heat_up[a] = jnp.where(low, pltpu.roll(prior[a], 4, 0), goal[a])


def heat_tiles(prior, goal, from_next, from_prev, a):
    low = sub_low()
    nxt, prv = from_next[a], from_prev[a]
    return (
        (prior[a], jnp.where(low, nxt, pltpu.roll(prv, 4, 0))),
        (goal[a], jnp.where(low, pltpu.roll(nxt, 4, 0), prv)),
    )


def rnext(v):
    return pltpu.roll(v, 15, 0)


def rprev(v):
    return pltpu.roll(v, 1, 0)


def lnext(v):
    return pltpu.roll(v, 255, 1)


def lprev(v):
    return pltpu.roll(v, 1, 1)


def magnetic_kernel(
    pot, fixed, spin, offs, halo, ring, ring_halo, current, reluct, eddy, loss,
    payload, misfit, weight, hring,
    wide, heat, hfield, region,
):
    find_region(fixed, spin, offs, region)
    low = sub_low()
    mains = [
        lambda at: pot[0, 0, at, :], lambda at: pot[1, 0, at, :], lambda at: pot[2, 0, at, :],
        lambda at: region[at, :], lambda at: ring[0, at, :], lambda at: ring[1, at, :],
    ]
    left, right = pl.ds(0, 128), pl.ds(128, 128)
    for n in range(6):
        source, f = (halo, n) if n < 4 else (ring_halo, n - 3)
        for t in range(32):
            wide[n, pl.ds(8 + 8 * t, 8), left] = mains[n](pl.ds(8 * t, 8))
            wide[n, pl.ds(8 + 8 * t, 8), right] = take(source[t // 4], 4 * (t % 4) + f)
        for side, block in ((left, source[8 + f]), (right, source[12 + f])):
            wide[n, pl.ds(264, 8), side] = jnp.where(low, block, 0.0)
            wide[n, pl.ds(0, 8), side] = jnp.where(low, 0.0, block)
            wide[n, pl.ds(272, 8), side] = jnp.zeros((8, 128), F32)
    for t in range(34):
        here, ahead = pl.ds(8 * t, 8), pl.ds(8 * t + 1, 8)
        pa, pr, pz = wide[0, here, :], wide[1, here, :], wide[2, here, :]
        fa = (wide[2, ahead, :] - pz) - (lnext(pr) - pr)
        fr = (lnext(pa) - pa) - (wide[5, here, :] - pz)
        fz = (wide[4, here, :] - pr) - (wide[0, ahead, :] - pa)
        rel, dens = lookup(wide[3, here, :], (reluct, loss))
        heat[t] = dens * (fa * fa + fr * fr + fz * fz)
        hfield[0, here, :] = rel * fa
        hfield[1, here, :] = rel * fr
        hfield[2, here, :] = rel * fz
        if 1 <= t <= 32:
            rows = pl.ds(8 * t - 8, 8)
            scale = 2.0 * dens
            for n, f in enumerate((fa, fr, fz)):
                weight[n, rows, :] = (scale * f)[:, :128]
            hring[0, rows, :] = (rel * fr)[:, :128]
            hring[1, rows, :] = (rel * fz)[:, :128]
    for t in range(1, 33):
        here, behind, rows = pl.ds(8 * t, 8), pl.ds(8 * t - 1, 8), pl.ds(8 * t - 8, 8)
        ha, hr, hz = hfield[0, here, :], hfield[1, here, :], hfield[2, here, :]
        ca = (lprev(hr) - hr) - (hfield[2, behind, :] - hz)
        cr = -hz - (lprev(ha) - ha)
        cz = (hfield[0, behind, :] - ha) + hr
        (sigma,) = lookup(region[rows, :], (eddy,))
        for n, c in enumerate((ca, cr, cz)):
            misfit[n, rows, :] = c[:, :128] + (sigma * pot[n, 0, rows, :] - current[n, 0, rows, :])
    for j in range(NA):
        t = j + 1
        packed = jnp.zeros((8, 128), F32)
        tiles = []
        for get in (lambda i: heat[i], lambda i: wide[3, pl.ds(8 * i, 8), :]):
            near, after, before = get(t), get(t + 1), get(t - 1)
            beyond = [jnp.where(low, after[:, k:k + 128], before[:, k:k + 128]) for k in (0, 128)]
            tiles.append((near[:, :128], near[:, 128:]))
            tiles.append(tuple(beyond))
        for c, (main, side) in enumerate(tiles):
            payload[j, pl.ds(8 * c, 8), :] = main
            packed = put(packed, c, side)
        payload[j, pl.ds(32, 8), :] = packed


def heat_kernel(
    got, prior, goal, from_next, from_prev, sides,
    plane, axial, storage, out,
    kin, kax, cap, pri, sens, src, coef, base, temp0, temp1, adj0, adj1,
):
    low = sub_low()

    def join(tiles, ends):
        return jnp.concatenate([jnp.concatenate(tiles, axis=0), jnp.concatenate(ends, axis=0)], axis=1)

    def gather(g, carry):
        inner = sides[NA + g]
        outer = jnp.where(low, from_next[NA + g], from_prev[NA + g])
        for u in range(8):
            a = 8 * g + u
            side = got[a, pl.ds(32, 8), :]
            tiles = [got[a, pl.ds(8 * c, 8), :] for c in range(4)]
            ends = [take(side, c) for c in range(4)]
            src[a] = join(tiles[:2], ends[:2])
            kin[a], kax[a], cap[a] = lookup(join(tiles[2:], ends[2:]), (plane, axial, storage))
            held = heat_tiles(prior, goal, from_next, from_prev, a)
            pri[a] = join(held[0], [take(inner, 2 * u), take(outer, 2 * u)])
            sens[a] = join(held[1], [take(inner, 2 * u + 1), take(outer, 2 * u + 1)])
        return carry

    lax.fori_loop(0, NA // 8, gather, 0)

    def prepare(a, carry):
        up = (a + 1) & (NA - 1)
        down = (a - 1) & (NA - 1)
        kp, ka, c = kin[a], kax[a], cap[a]
        source = c * pri[a] + src[a]
        w = [
            0.5 * (kp + kin[up]), 0.5 * (kp + kin[down]),
            0.5 * (kp + rnext(kp)), 0.5 * (kp + rprev(kp)),
            0.5 * (ka + lnext(ka)), 0.5 * (ka + lprev(ka)),
        ]
        total = c + (((((w[0] + w[1]) + w[2]) + w[3]) + w[4]) + w[5])
        inside = c > 0.0
        inv = jnp.where(inside, 1.0 / jnp.where(inside, total, 1.0), 0.0)
        for n in range(6):
            coef[n, a] = inv * w[n]
        base[0, a] = inv * source
        first = inv * sens[a]
        base[1, a] = first
        adj0[a] = first
        return carry

    lax.fori_loop(0, NA, prepare, 0, unroll=16)

    def relax(field, a, c, b):
        up = (a + 1) & (NA - 1)
        down = (a - 1) & (NA - 1)
        v = field[a]
        total = b + c[0] * field[up] + c[1] * field[down]
        total = total + c[2] * rnext(v) + c[3] * rprev(v)
        return total + c[4] * lnext(v) + c[5] * lprev(v)

    temps = [pri, temp0, temp1, temp0, temp1]
    adjs = [None, adj0, adj1, adj0, adj1]
    for sweep in range(SWEEPS):

        def step(a, carry, sweep=sweep):
            c = [coef[n, a] for n in range(6)]
            t = relax(temps[sweep], a, c, base[0, a])
            if sweep == SWEEPS - 1:
                out[a, pl.ds(0, 8), :] = t[:8, :128]
            else:
                temps[sweep + 1][a] = t
            if sweep > 0:
                s = relax(adjs[sweep], a, c, base[1, a])
                if sweep == SWEEPS - 1:
                    out[a, pl.ds(8, 8), :] = s[:8, :128]
                else:
                    adjs[sweep + 1][a] = s
            return carry

        lax.fori_loop(0, NA, step, 0, unroll=32)


def finish_kernel(got, part, weight, hring, misfit, dual, state):
    misfit[0, 0] = part[0]
    misfit[1, 0] = part[1] + hring[1]
    misfit[2, 0] = part[2] - hring[0]

    def step(j, carry):
        at = pl.ds(pl.multiple_of(8 * j, 8), 8)
        state[0, at, :] = got[j, pl.ds(0, 8), :]
        adjoint = got[j, pl.ds(8, 8), :]
        for f in range(3):
            dual[f, 0, at, :] = weight[f, at, :] * adjoint
        return carry

    lax.fori_loop(0, NA, step, 0, unroll=8)


def body(
    magnetic_vector_field,
    imposed_current_density,
    fixed_material_map,
    spinning_material_map,
    slab_slide_offsets,
    inverse_permeability,
    electric_conductance,
    core_dissipation_coefficient,
    inplane_thermal_conductance,
    through_plane_conductance,
    thermal_storage,
    prior_thermal_state,
    goal_sensitivity,
):
    rows = lax.axis_size("section") * lax.axis_size("azim")
    chain = ("section", "azim")
    onward = [(i, i + 1) for i in range(rows - 1)]
    backward = [(i + 1, i) for i in range(rows - 1)]
    from_after = [((i + 1) % NA, i) for i in range(NA)]
    from_before = [(i, (i + 1) % NA) for i in range(NA)]

    offsets = slab_slide_offsets.reshape(1, 128)
    maps = (fixed_material_map, spinning_material_map, offsets)
    row_edge, frame, ring = pl.pallas_call(
        send_kernel,
        out_shape=(pltpu.VMEM((4, 8, 128), F32), pltpu.VMEM((12, 8, 128), F32), pltpu.VMEM((2, 256, 128), F32)),
        in_specs=[HBM] * 6,
        out_specs=(VM,) * 3,
        scratch_shapes=[
            pltpu.VMEM((3, 1, 256, 128), F32),
            pltpu.VMEM((1, 256, 128), jnp.int32),
            pltpu.VMEM((NA, 128), jnp.int32),
            pltpu.VMEM((1, 128), jnp.int32),
            pltpu.VMEM((NA, 8, 128), F32),
            pltpu.VMEM((NA, 8, 128), F32),
            pltpu.VMEM((256, 128), F32),
            pltpu.SemaphoreType.DMA((6,)),
        ],
        compiler_params=params(56),
        name="send",
    )(magnetic_vector_field, *maps, prior_thermal_state, goal_sensitivity)
    across = lax.ppermute(row_edge, "section", [(0, 1), (1, 0)])
    ring_main = lax.ppermute(ring, "azim", from_after)
    frame = pl.pallas_call(
        frame_kernel, out_shape=struct(16, 8, 128), in_specs=[VM] * 2, out_specs=VM,
        compiler_params=params(8), name="frame",
    )(frame, across)
    core = lax.ppermute(frame, "axial", [(0, 1), (1, 0), (2, 3), (3, 2)])
    far = lax.ppermute(frame, "axial", [(1, 2), (2, 1)])
    halo, heat_down, heat_up = pl.pallas_call(
        halo_kernel,
        out_shape=(struct(16, 8, 128), struct(NA + 4, 8, 128), struct(NA + 4, 8, 128)),
        in_specs=[VM] * 5,
        out_specs=(VM,) * 3,
        compiler_params=params(8),
        name="halo",
    )(frame, core, far, prior_thermal_state, goal_sensitivity)
    ring_halo = lax.ppermute(halo, "azim", from_after)
    payload, part, weight, hring = pl.pallas_call(
        magnetic_kernel,
        out_shape=(pltpu.VMEM((NA, 40, 128), F32), struct(3, 256, 128), struct(3, 256, 128), struct(2, 256, 128)),
        in_specs=[VM] * 8 + [SM] * 3,
        out_specs=(VM,) * 4,
        scratch_shapes=[
            pltpu.VMEM((6, 280, 256), F32),
            pltpu.VMEM((34, 8, 256), F32),
            pltpu.VMEM((3, 272, 256), F32),
            pltpu.VMEM((256, 128), F32),
        ],
        compiler_params=params(24),
        name="magnetic",
    )(
        magnetic_vector_field, *maps, halo, ring_main, ring_halo, imposed_current_density,
        inverse_permeability, electric_conductance, core_dissipation_coefficient,
    )
    heat_prev = lax.ppermute(heat_up, chain, onward)
    heat_next = lax.ppermute(heat_down, chain, backward)
    hring = lax.ppermute(hring, "azim", from_before)
    got = lax.all_to_all(payload, "azim", split_axis=0, concat_axis=0, tiled=True)
    wide = pltpu.VMEM((NA, 16, 256), F32)
    result = pl.pallas_call(
        heat_kernel,
        out_shape=pltpu.VMEM((NA, 16, 128), F32),
        in_specs=[VM] * 6 + [SM] * 3,
        out_specs=VM,
        scratch_shapes=[
            wide, wide, wide, wide, wide, wide,
            pltpu.VMEM((6, NA, 16, 256), F32),
            pltpu.VMEM((2, NA, 16, 256), F32),
            wide, wide, wide, wide,
        ],
        compiler_params=params(32),
        cost_estimate=pl.CostEstimate(flops=20_000_000, bytes_accessed=20_000_000, transcendentals=0),
        name="heat",
    )(
        got, prior_thermal_state, goal_sensitivity, heat_next, heat_prev, heat_down,
        inplane_thermal_conductance, through_plane_conductance, thermal_storage,
    )
    result, hring = lax.optimization_barrier((result, hring))
    back = lax.all_to_all(result, "azim", split_axis=0, concat_axis=0, tiled=True)
    return pl.pallas_call(
        finish_kernel,
        out_shape=(struct(3, 1, 256, 128), struct(3, 1, 256, 128), struct(1, 256, 128)),
        in_specs=[VM] * 4,
        out_specs=(VM,) * 3,
        compiler_params=params(16),
        name="finish",
    )(back, part, weight, hring)


def solution(mesh):
    in_specs = (
        P(None, "azim", "section", "axial"),
        P(None, "azim", "section", "axial"),
        P("azim", "section", "axial"),
        P(),
        P("axial"),
        P(),
        P(),
        P(),
        P(),
        P(),
        P(),
        P(None, ("section", "azim"), "axial"),
        P(None, ("section", "azim"), "axial"),
    )
    out_specs = (
        P(None, "azim", "section", "axial"),
        P(None, "azim", "section", "axial"),
        P("azim", "section", "axial"),
    )
    return jax.shard_map(body, mesh=mesh, in_specs=in_specs, out_specs=out_specs, check_vma=False)
```

```python
import jax
import jax.numpy as jnp
from jax import lax
from jax.experimental import pallas as pl
from jax.experimental.pallas import tpu as pltpu
from jax.sharding import PartitionSpec as P

NREG = 8
SWEEPS = 4
NA = 32
F32 = jnp.float32
VM = pl.BlockSpec(memory_space=pltpu.VMEM)
SM = pl.BlockSpec(memory_space=pltpu.SMEM)
HBM = pl.BlockSpec(memory_space=pltpu.HBM)


def params(mib):
    return pltpu.CompilerParams(vmem_limit_bytes=mib * 1024 * 1024)


def struct(*shape):
    return jax.ShapeDtypeStruct(shape, F32)


def sub_low():
    return lax.broadcasted_iota(jnp.int32, (8, 128), 0) < 4


def lanes():
    return lax.broadcasted_iota(jnp.int32, (8, 128), 1)


def put(packed, slot, tile):
    return jnp.where(lanes() // 8 == slot, pltpu.roll(tile, 4 + 8 * slot, 1), packed)


def take(packed, slot):
    lane = lanes()
    return jnp.where((lane < 4) | (lane >= 124), pltpu.roll(packed, 124 - 8 * slot, 1), 0.0)


def lookup(region, tables):
    found = [jnp.zeros(region.shape, F32) for _ in tables]
    for k in range(NREG):
        match = region == float(k + 1)
        found = [jnp.where(match, t[k], f) for t, f in zip(tables, found)]
    return found


def find_region(fixed, spin, offs, region):
    section = lax.axis_index("section")
    azim = lax.axis_index("azim")
    shifted = (azim - offs[...]) & (NA - 1)
    rows = lax.broadcasted_iota(jnp.int32, (NA, 128), 0)
    hot = jnp.where(rows == shifted, 1.0, 0.0).astype(jnp.bfloat16)
    rotor = lax.dot_general(
        spin[...].astype(F32).astype(jnp.bfloat16), hot, (((0,), (0,)), ((), ())), preferred_element_type=F32
    )
    stator = fixed[0].astype(F32)
    region[:128] = jnp.where(section == 0, rotor, stator[:128]) + 1.0
    region[128:] = stator[128:] + 1.0


def send_kernel(
    pot_in, fixed_in, spin_in, offs_in, prior_in, goal_in,
    row_edge, edge, ring, planes,
    pot, fixed, spin, offs, prior, goal, region, sems,
):
    pairs = ((pot_in, pot), (fixed_in, fixed), (spin_in, spin), (offs_in, offs), (prior_in, prior), (goal_in, goal))
    copies = [pltpu.make_async_copy(src, dst, sems.at[n]) for n, (src, dst) in enumerate(pairs)]
    for copy in copies:
        copy.start()
    for copy in copies[1:4]:
        copy.wait()
    find_region(fixed, spin, offs, region)
    copies[0].wait()
    low = sub_low()

    def tile(f, t):
        at = pl.ds(8 * t, 8)
        return region[at, :] if f == 3 else pot[f, 0, at, :]

    for f in range(4):
        row_edge[f] = jnp.where(low, tile(f, 0), tile(f, 31))
    for g in range(8):
        packed = jnp.zeros((8, 128), F32)
        for u in range(4):
            for f in range(4):
                packed = put(packed, 4 * u + f, tile(f, 4 * g + u))
        edge[g] = packed
    ring[0] = pot[1, 0]
    ring[1] = pot[2, 0]
    for f in range(3):
        planes[f] = pot[f, 0]
    planes[3] = region[...]
    copies[4].wait()
    copies[5].wait()
    for g in range(4):
        packed = jnp.zeros((8, 128), F32)
        for u in range(8):
            packed = put(packed, 2 * u, prior[8 * g + u])
            packed = put(packed, 2 * u + 1, goal[8 * g + u])
        edge[8 + g] = packed


def frame_kernel(edge, across, out):
    valid = sub_low() == (lax.axis_index("section") == 0)
    for g in range(12):
        out[g] = edge[g]
    for f in range(4):
        out[12 + f] = jnp.where(valid, across[f], 0.0)


def halo_kernel(own, core, far, prior, goal, halo, heat_down, heat_up):
    odd = lax.axis_index("axial") % 2 == 1
    lane = lanes()
    low = sub_low()
    right = lane % 8 >= 4
    for g in range(16):
        after = jnp.where(odd, far[g], core[g])
        before = jnp.where(odd, core[g], far[g])
        if g < 8:
            halo[g] = jnp.where(right, after, before)
        elif g < 12:
            merged = jnp.where(right, after, before)
            heat_down[24 + g] = merged
            heat_up[24 + g] = merged
        else:
            halo[g - 4] = own[g]
            halo[g] = jnp.where(lane < 4, after, jnp.where(lane >= 124, before, 0.0))
    for a in range(NA):
        heat_down[a] = jnp.where(low, prior[a], pltpu.roll(goal[a], 4, 0))
        heat_up[a] = jnp.where(low, pltpu.roll(prior[a], 4, 0), goal[a])


def heat_tiles(prior, goal, from_next, from_prev, a):
    low = sub_low()
    nxt, prv = from_next[a], from_prev[a]
    return (
        (prior[a], jnp.where(low, nxt, pltpu.roll(prv, 4, 0))),
        (goal[a], jnp.where(low, pltpu.roll(nxt, 4, 0), prv)),
    )


def rnext(v):
    return pltpu.roll(v, 15, 0)


def rprev(v):
    return pltpu.roll(v, 1, 0)


def lnext(v):
    return pltpu.roll(v, 255, 1)


def lprev(v):
    return pltpu.roll(v, 1, 1)


def widen(wide, n, main, halo, f):
    low = sub_low()
    left, right = pl.ds(0, 128), pl.ds(128, 128)
    for t in range(32):
        wide[n, pl.ds(8 + 8 * t, 8), left] = main(pl.ds(8 * t, 8))
        wide[n, pl.ds(8 + 8 * t, 8), right] = take(halo[t // 4], 4 * (t % 4) + f)
    for side, block in ((left, halo[8 + f]), (right, halo[12 + f])):
        wide[n, pl.ds(264, 8), side] = jnp.where(low, block, 0.0)
        wide[n, pl.ds(0, 8), side] = jnp.where(low, 0.0, block)
        wide[n, pl.ds(272, 8), side] = jnp.zeros((8, 128), F32)


def fluxes(wide, t):
    here, ahead = pl.ds(8 * t, 8), pl.ds(8 * t + 1, 8)
    pa, pr, pz = wide[0, here, :], wide[1, here, :], wide[2, here, :]
    fa = (wide[2, ahead, :] - pz) - (lnext(pr) - pr)
    fr = (lnext(pa) - pa) - (wide[5, here, :] - pz)
    fz = (wide[4, here, :] - pr) - (wide[0, ahead, :] - pa)
    return fa, fr, fz


def widen_all(wide, pot, region, halo, ring, halo_after):
    for f in range(3):
        widen(wide, f, lambda at, f=f: pot[f, 0, at, :], halo, f)
    widen(wide, 3, lambda at: region[at, :], halo, 3)
    for n in range(2):
        widen(wide, 4 + n, lambda at, n=n: ring[n, at, :], halo_after, 1 + n)


def magnetic_kernel(
    pot, fixed, spin, offs, halo, ring, halo_after, loss,
    payload,
    wide, heat, region,
):
    find_region(fixed, spin, offs, region)
    widen_all(wide, pot, region, halo, ring, halo_after)
    low = sub_low()
    for t in range(34):
        fa, fr, fz = fluxes(wide, t)
        (dens,) = lookup(wide[3, pl.ds(8 * t, 8), :], (loss,))
        heat[t] = dens * (fa * fa + fr * fr + fz * fz)
    for j in range(NA):
        t = j + 1
        tiles = []
        for get in (lambda i: heat[i], lambda i: wide[3, pl.ds(8 * i, 8), :]):
            near, after, before = get(t), get(t + 1), get(t - 1)
            beyond = [jnp.where(low, after[:, k:k + 128], before[:, k:k + 128]) for k in (0, 128)]
            tiles.append((near[:, :128], near[:, 128:]))
            tiles.append(tuple(beyond))
        packed = jnp.zeros((8, 128), F32)
        for c in range(4):
            payload[j, pl.ds(8 * c, 8), :] = tiles[c][0]
            packed = put(packed, c, tiles[c][1])
        payload[j, pl.ds(32, 8), :] = packed


def curl_kernel(
    pot, fixed, spin, offs, halo, ring, halo_after, planes, halo_before, current, reluct, eddy, loss,
    misfit, weight,
    wide, hfield, region,
):
    find_region(fixed, spin, offs, region)
    widen_all(wide, pot, region, halo, ring, halo_after)
    widen(wide, 6, lambda at: planes[0, at, :], halo_before, 0)
    for t in range(34):
        here, rows = pl.ds(8 * t, 8), pl.ds(8 * t - 8, 8)
        fa, fr, fz = fluxes(wide, t)
        rel, dens = lookup(wide[3, here, :], (reluct, loss))
        hfield[0, here, :] = rel * fa
        hfield[1, here, :] = rel * fr
        hfield[2, here, :] = rel * fz
        if 1 <= t <= 32:
            scale = 2.0 * dens
            for n, f in enumerate((fa, fr, fz)):
                weight[n, rows, :] = (scale * f)[:, :128]
    for t in range(1, 33):
        here, ahead, behind, rows = pl.ds(8 * t, 8), pl.ds(8 * t + 1, 8), pl.ds(8 * t - 1, 8), pl.ds(8 * t - 8, 8)
        ha, hr, hz = hfield[0, here, :], hfield[1, here, :], hfield[2, here, :]
        before = wide[6, here, :]
        (rel,) = lookup(planes[3, rows, :], (reluct,))
        hr_before = rel * ((lnext(before) - before)[:, :128] - (pot[2, 0, rows, :] - planes[2, rows, :]))
        hz_before = rel * ((pot[1, 0, rows, :] - planes[1, rows, :]) - (wide[6, ahead, :] - before)[:, :128])
        ca = ((lprev(hr) - hr) - (hfield[2, behind, :] - hz))[:, :128]
        cr = (hz_before - hz[:, :128]) - (lprev(ha) - ha)[:, :128]
        cz = (hfield[0, behind, :] - ha)[:, :128] - (hr_before - hr[:, :128])
        (sigma,) = lookup(region[rows, :], (eddy,))
        for n, c in enumerate((ca, cr, cz)):
            misfit[n, 0, rows, :] = c + sigma * pot[n, 0, rows, :] - current[n, 0, rows, :]


def heat_kernel(
    got, prior, goal, from_next, from_prev, sides,
    plane, axial, storage, out,
    kin, kax, cap, pri, sens, src, coef, base, temp0, temp1, adj0, adj1,
):
    low = sub_low()

    def join(tiles, ends):
        return jnp.concatenate([jnp.concatenate(tiles, axis=0), jnp.concatenate(ends, axis=0)], axis=1)

    def gather(g, carry):
        inner = sides[NA + g]
        outer = jnp.where(low, from_next[NA + g], from_prev[NA + g])
        for u in range(8):
            a = 8 * g + u
            tiles = [got[a, pl.ds(8 * c, 8), :] for c in range(4)]
            side = got[a, pl.ds(32, 8), :]
            ends = [take(side, c) for c in range(4)]
            src[a] = join(tiles[:2], ends[:2])
            kin[a], kax[a], cap[a] = lookup(join(tiles[2:], ends[2:]), (plane, axial, storage))
            held = heat_tiles(prior, goal, from_next, from_prev, a)
            pri[a] = join(held[0], [take(inner, 2 * u), take(outer, 2 * u)])
            sens[a] = join(held[1], [take(inner, 2 * u + 1), take(outer, 2 * u + 1)])
        return carry

    lax.fori_loop(0, NA // 8, gather, 0)

    def prepare(a, carry):
        up = (a + 1) & (NA - 1)
        down = (a - 1) & (NA - 1)
        kp, ka, c = kin[a], kax[a], cap[a]
        source = c * pri[a] + src[a]
        w = [
            0.5 * (kp + kin[up]), 0.5 * (kp + kin[down]),
            0.5 * (kp + rnext(kp)), 0.5 * (kp + rprev(kp)),
            0.5 * (ka + lnext(ka)), 0.5 * (ka + lprev(ka)),
        ]
        total = c + (((((w[0] + w[1]) + w[2]) + w[3]) + w[4]) + w[5])
        inside = c > 0.0
        inv = jnp.where(inside, 1.0 / jnp.where(inside, total, 1.0), 0.0)
        for n in range(6):
            coef[n, a] = inv * w[n]
        base[0, a] = inv * source
        first = inv * sens[a]
        base[1, a] = first
        adj0[a] = first
        return carry

    lax.fori_loop(0, NA, prepare, 0, unroll=16)

    def relax(field, a, c, b):
        up = (a + 1) & (NA - 1)
        down = (a - 1) & (NA - 1)
        v = field[a]
        total = b + c[0] * field[up] + c[1] * field[down]
        total = total + c[2] * rnext(v) + c[3] * rprev(v)
        return total + c[4] * lnext(v) + c[5] * lprev(v)

    temps = [pri, temp0, temp1, temp0, temp1]
    adjs = [None, adj0, adj1, adj0, adj1]
    for sweep in range(SWEEPS):

        def step(a, carry, sweep=sweep):
            c = [coef[n, a] for n in range(6)]
            t = relax(temps[sweep], a, c, base[0, a])
            if sweep == SWEEPS - 1:
                out[a, pl.ds(0, 8), :] = t[:8, :128]
            else:
                temps[sweep + 1][a] = t
            if sweep > 0:
                s = relax(adjs[sweep], a, c, base[1, a])
                if sweep == SWEEPS - 1:
                    out[a, pl.ds(8, 8), :] = s[:8, :128]
                else:
                    adjs[sweep + 1][a] = s
            return carry

        lax.fori_loop(0, NA, step, 0, unroll=32)


def finish_kernel(got, weight, dual, state):
    def step(j, carry):
        at = pl.ds(pl.multiple_of(8 * j, 8), 8)
        state[0, at, :] = got[j, pl.ds(0, 8), :]
        adjoint = got[j, pl.ds(8, 8), :]
        for f in range(3):
            dual[f, 0, at, :] = weight[f, at, :] * adjoint
        return carry

    lax.fori_loop(0, NA, step, 0, unroll=8)


def body(
    magnetic_vector_field,
    imposed_current_density,
    fixed_material_map,
    spinning_material_map,
    slab_slide_offsets,
    inverse_permeability,
    electric_conductance,
    core_dissipation_coefficient,
    inplane_thermal_conductance,
    through_plane_conductance,
    thermal_storage,
    prior_thermal_state,
    goal_sensitivity,
):
    rows = lax.axis_size("section") * lax.axis_size("azim")
    chain = ("section", "azim")
    onward = [(i, i + 1) for i in range(rows - 1)]
    backward = [(i + 1, i) for i in range(rows - 1)]
    from_after = [((i + 1) % NA, i) for i in range(NA)]
    from_before = [(i, (i + 1) % NA) for i in range(NA)]

    offsets = slab_slide_offsets.reshape(1, 128)
    maps = (fixed_material_map, spinning_material_map, offsets)
    row_edge, edge, ring, planes = pl.pallas_call(
        send_kernel,
        out_shape=tuple(pltpu.VMEM(d, F32) for d in ((4, 8, 128), (12, 8, 128), (2, 256, 128), (4, 256, 128))),
        in_specs=[HBM] * 6,
        out_specs=(VM,) * 4,
        scratch_shapes=[
            pltpu.VMEM((3, 1, 256, 128), F32),
            pltpu.VMEM((1, 256, 128), jnp.int32),
            pltpu.VMEM((NA, 128), jnp.int32),
            pltpu.VMEM((1, 128), jnp.int32),
            pltpu.VMEM((NA, 8, 128), F32),
            pltpu.VMEM((NA, 8, 128), F32),
            pltpu.VMEM((256, 128), F32),
            pltpu.SemaphoreType.DMA((6,)),
        ],
        compiler_params=params(56),
        name="send",
    )(magnetic_vector_field, *maps, prior_thermal_state, goal_sensitivity)
    across = lax.ppermute(row_edge, "section", [(0, 1), (1, 0)])
    frame = pl.pallas_call(
        frame_kernel, out_shape=struct(16, 8, 128), in_specs=[VM] * 2, out_specs=VM,
        compiler_params=params(8), name="frame",
    )(edge, across)
    frame, ring, planes = lax.optimization_barrier((frame, ring, planes))
    ring = lax.ppermute(ring, "azim", from_after)
    planes = lax.ppermute(planes, "azim", from_before)
    core = lax.ppermute(frame, "axial", [(0, 1), (1, 0), (2, 3), (3, 2)])
    far = lax.ppermute(frame, "axial", [(1, 2), (2, 1)])
    halo, heat_down, heat_up = pl.pallas_call(
        halo_kernel,
        out_shape=(struct(16, 8, 128), struct(NA + 4, 8, 128), struct(NA + 4, 8, 128)),
        in_specs=[VM] * 5,
        out_specs=(VM,) * 3,
        compiler_params=params(8),
        name="halo",
    )(frame, core, far, prior_thermal_state, goal_sensitivity)
    halo_after = lax.ppermute(halo, "azim", from_after)
    block = (magnetic_vector_field, *maps, halo, ring, halo_after)
    payload = pl.pallas_call(
        magnetic_kernel,
        out_shape=pltpu.VMEM((NA, 40, 128), F32),
        in_specs=[VM] * 7 + [SM],
        out_specs=VM,
        scratch_shapes=[
            pltpu.VMEM((6, 280, 256), F32),
            pltpu.VMEM((34, 8, 256), F32),
            pltpu.VMEM((256, 128), F32),
        ],
        compiler_params=params(24),
        name="magnetic",
    )(*block, core_dissipation_coefficient)
    halo_before = lax.ppermute(halo, "azim", from_before)
    payload, planes, halo_before = lax.optimization_barrier((payload, planes, halo_before))
    got = lax.all_to_all(payload, "azim", split_axis=0, concat_axis=0, tiled=True)
    heat_prev = lax.ppermute(heat_up, chain, onward)
    heat_next = lax.ppermute(heat_down, chain, backward)
    misfit, weight = pl.pallas_call(
        curl_kernel,
        out_shape=(struct(3, 1, 256, 128), struct(3, 256, 128)),
        in_specs=[VM] * 10 + [SM] * 3,
        out_specs=(VM, VM),
        scratch_shapes=[
            pltpu.VMEM((7, 280, 256), F32),
            pltpu.VMEM((3, 272, 256), F32),
            pltpu.VMEM((256, 128), F32),
        ],
        compiler_params=params(24),
        cost_estimate=pl.CostEstimate(flops=10_000_000, bytes_accessed=10_000_000, transcendentals=0),
        name="curl",
    )(
        *block, planes, halo_before, imposed_current_density,
        inverse_permeability, electric_conductance, core_dissipation_coefficient,
    )
    wide = pltpu.VMEM((NA, 16, 256), F32)
    result = pl.pallas_call(
        heat_kernel,
        out_shape=pltpu.VMEM((NA, 16, 128), F32),
        in_specs=[VM] * 6 + [SM] * 3,
        out_specs=VM,
        scratch_shapes=[
            wide, wide, wide, wide, wide, wide,
            pltpu.VMEM((6, NA, 16, 256), F32),
            pltpu.VMEM((2, NA, 16, 256), F32),
            wide, wide, wide, wide,
        ],
        compiler_params=params(32),
        cost_estimate=pl.CostEstimate(flops=20_000_000, bytes_accessed=20_000_000, transcendentals=0),
        name="heat",
    )(
        got, prior_thermal_state, goal_sensitivity, heat_next, heat_prev, heat_down,
        inplane_thermal_conductance, through_plane_conductance, thermal_storage,
    )
    back = lax.all_to_all(result, "azim", split_axis=0, concat_axis=0, tiled=True)
    dual, state = pl.pallas_call(
        finish_kernel,
        out_shape=(struct(3, 1, 256, 128), struct(1, 256, 128)),
        in_specs=[VM] * 2,
        out_specs=(VM,) * 2,
        compiler_params=params(16),
        name="finish",
    )(back, weight)
    return misfit, dual, state


def solution(mesh):
    in_specs = (
        P(None, "azim", "section", "axial"),
        P(None, "azim", "section", "axial"),
        P("azim", "section", "axial"),
        P(),
        P("axial"),
        P(),
        P(),
        P(),
        P(),
        P(),
        P(),
        P(None, ("section", "azim"), "axial"),
        P(None, ("section", "azim"), "axial"),
    )
    out_specs = (
        P(None, "azim", "section", "axial"),
        P(None, "azim", "section", "axial"),
        P("azim", "section", "axial"),
    )
    return jax.shard_map(body, mesh=mesh, in_specs=in_specs, out_specs=out_specs, check_vma=False)
```

```python
import jax
import jax.numpy as jnp
from jax import lax
from jax.experimental import pallas as pl
from jax.experimental.pallas import tpu as pltpu
from jax.sharding import PartitionSpec as P

NREG = 8
SWEEPS = 4
NA = 32
F32 = jnp.float32
VM = pl.BlockSpec(memory_space=pltpu.VMEM)
SM = pl.BlockSpec(memory_space=pltpu.SMEM)
HBM = pl.BlockSpec(memory_space=pltpu.HBM)


def params(mib):
    return pltpu.CompilerParams(vmem_limit_bytes=mib * 1024 * 1024)


def struct(*shape):
    return jax.ShapeDtypeStruct(shape, F32)


def sub_low():
    return lax.broadcasted_iota(jnp.int32, (8, 128), 0) < 4


def lanes():
    return lax.broadcasted_iota(jnp.int32, (8, 128), 1)


def put(packed, slot, tile):
    return jnp.where(lanes() // 8 == slot, pltpu.roll(tile, 4 + 8 * slot, 1), packed)


def take(packed, slot):
    lane = lanes()
    return jnp.where((lane < 4) | (lane >= 124), pltpu.roll(packed, 124 - 8 * slot, 1), 0.0)


def lookup(region, tables):
    found = [jnp.zeros(region.shape, F32) for _ in tables]
    for k in range(NREG):
        match = region == float(k + 1)
        found = [jnp.where(match, t[k], f) for t, f in zip(tables, found)]
    return found


def find_region(fixed, spin, offs, region):
    section = lax.axis_index("section")
    azim = lax.axis_index("azim")
    shifted = (azim - offs[...]) & (NA - 1)
    rows = lax.broadcasted_iota(jnp.int32, (NA, 128), 0)
    hot = jnp.where(rows == shifted, 1.0, 0.0).astype(jnp.bfloat16)
    rotor = lax.dot_general(
        spin[...].astype(F32).astype(jnp.bfloat16), hot, (((0,), (0,)), ((), ())), preferred_element_type=F32
    )
    stator = fixed[0].astype(F32)
    region[:128] = jnp.where(section == 0, rotor, stator[:128]) + 1.0
    region[128:] = stator[128:] + 1.0


def send_kernel(
    pot_in, fixed_in, spin_in, offs_in, prior_in, goal_in,
    row_edge, edge, ring, planes,
    pot, fixed, spin, offs, prior, goal, region, sems,
):
    pairs = ((pot_in, pot), (fixed_in, fixed), (spin_in, spin), (offs_in, offs), (prior_in, prior), (goal_in, goal))
    copies = [pltpu.make_async_copy(src, dst, sems.at[n]) for n, (src, dst) in enumerate(pairs)]
    for copy in copies:
        copy.start()
    for copy in copies[1:4]:
        copy.wait()
    find_region(fixed, spin, offs, region)
    copies[0].wait()
    low = sub_low()

    def tile(f, t):
        at = pl.ds(8 * t, 8)
        return region[at, :] if f == 3 else pot[f, 0, at, :]

    for f in range(4):
        row_edge[f] = jnp.where(low, tile(f, 0), tile(f, 31))
    for g in range(8):
        packed = jnp.zeros((8, 128), F32)
        for u in range(4):
            for f in range(4):
                packed = put(packed, 4 * u + f, tile(f, 4 * g + u))
        edge[g] = packed
    ring[0] = pot[1, 0]
    ring[1] = pot[2, 0]
    for f in range(3):
        planes[f] = pot[f, 0]
    planes[3] = region[...]
    copies[4].wait()
    copies[5].wait()
    for g in range(4):
        packed = jnp.zeros((8, 128), F32)
        for u in range(8):
            packed = put(packed, 2 * u, prior[8 * g + u])
            packed = put(packed, 2 * u + 1, goal[8 * g + u])
        edge[8 + g] = packed


def frame_kernel(edge, across, out):
    valid = sub_low() == (lax.axis_index("section") == 0)
    for g in range(12):
        out[g] = edge[g]
    for f in range(4):
        out[12 + f] = jnp.where(valid, across[f], 0.0)


def halo_kernel(own, core, far, prior, goal, halo, heat_down, heat_up):
    odd = lax.axis_index("axial") % 2 == 1
    lane = lanes()
    low = sub_low()
    right = lane % 8 >= 4
    for g in range(16):
        after = jnp.where(odd, far[g], core[g])
        before = jnp.where(odd, core[g], far[g])
        if g < 8:
            halo[g] = jnp.where(right, after, before)
        elif g < 12:
            merged = jnp.where(right, after, before)
            heat_down[24 + g] = merged
            heat_up[24 + g] = merged
        else:
            halo[g - 4] = own[g]
            halo[g] = jnp.where(lane < 4, after, jnp.where(lane >= 124, before, 0.0))
    for a in range(NA):
        heat_down[a] = jnp.where(low, prior[a], pltpu.roll(goal[a], 4, 0))
        heat_up[a] = jnp.where(low, pltpu.roll(prior[a], 4, 0), goal[a])


def heat_tiles(prior, goal, from_next, from_prev, a):
    low = sub_low()
    nxt, prv = from_next[a], from_prev[a]
    return (
        (prior[a], jnp.where(low, nxt, pltpu.roll(prv, 4, 0))),
        (goal[a], jnp.where(low, pltpu.roll(nxt, 4, 0), prv)),
    )


def rnext(v):
    return pltpu.roll(v, 15, 0)


def rprev(v):
    return pltpu.roll(v, 1, 0)


def lnext(v):
    return pltpu.roll(v, 255, 1)


def lprev(v):
    return pltpu.roll(v, 1, 1)


def widen(wide, n, main, halo, f):
    low = sub_low()
    left, right = pl.ds(0, 128), pl.ds(128, 128)
    for t in range(32):
        wide[n, pl.ds(8 + 8 * t, 8), left] = main(pl.ds(8 * t, 8))
        wide[n, pl.ds(8 + 8 * t, 8), right] = take(halo[t // 4], 4 * (t % 4) + f)
    for side, block in ((left, halo[8 + f]), (right, halo[12 + f])):
        wide[n, pl.ds(264, 8), side] = jnp.where(low, block, 0.0)
        wide[n, pl.ds(0, 8), side] = jnp.where(low, 0.0, block)
        wide[n, pl.ds(272, 8), side] = jnp.zeros((8, 128), F32)


def fluxes(wide, t):
    here, ahead = pl.ds(8 * t, 8), pl.ds(8 * t + 1, 8)
    pa, pr, pz = wide[0, here, :], wide[1, here, :], wide[2, here, :]
    fa = (wide[2, ahead, :] - pz) - (lnext(pr) - pr)
    fr = (lnext(pa) - pa) - (wide[5, here, :] - pz)
    fz = (wide[4, here, :] - pr) - (wide[0, ahead, :] - pa)
    return fa, fr, fz


def widen_all(wide, pot, region, halo, ring, halo_after):
    for f in range(3):
        widen(wide, f, lambda at, f=f: pot[f, 0, at, :], halo, f)
    widen(wide, 3, lambda at: region[at, :], halo, 3)
    for n in range(2):
        widen(wide, 4 + n, lambda at, n=n: ring[n, at, :], halo_after, 1 + n)


def magnetic_kernel(
    pot, fixed, spin, offs, halo, ring, halo_after, loss,
    payload,
    wide, heat, region,
):
    find_region(fixed, spin, offs, region)
    widen_all(wide, pot, region, halo, ring, halo_after)
    low = sub_low()
    for t in range(34):
        fa, fr, fz = fluxes(wide, t)
        (dens,) = lookup(wide[3, pl.ds(8 * t, 8), :], (loss,))
        heat[t] = dens * (fa * fa + fr * fr + fz * fz)
    for j in range(NA):
        t = j + 1
        tiles = []
        for get in (lambda i: heat[i], lambda i: wide[3, pl.ds(8 * i, 8), :]):
            near, after, before = get(t), get(t + 1), get(t - 1)
            beyond = [jnp.where(low, after[:, k:k + 128], before[:, k:k + 128]) for k in (0, 128)]
            tiles.append((near[:, :128], near[:, 128:]))
            tiles.append(tuple(beyond))
        packed = jnp.zeros((8, 128), F32)
        for c in range(4):
            payload[j, pl.ds(8 * c, 8), :] = tiles[c][0]
            packed = put(packed, c, tiles[c][1])
        payload[j, pl.ds(32, 8), :] = packed


def curl_kernel(
    pot, fixed, spin, offs, halo, ring, halo_after, planes, halo_before, current, reluct, eddy, loss,
    misfit, weight,
    wide, hfield, region,
):
    find_region(fixed, spin, offs, region)
    widen_all(wide, pot, region, halo, ring, halo_after)
    widen(wide, 6, lambda at: planes[0, at, :], halo_before, 0)
    for t in range(34):
        here, rows = pl.ds(8 * t, 8), pl.ds(8 * t - 8, 8)
        fa, fr, fz = fluxes(wide, t)
        rel, dens = lookup(wide[3, here, :], (reluct, loss))
        hfield[0, here, :] = rel * fa
        hfield[1, here, :] = rel * fr
        hfield[2, here, :] = rel * fz
        if 1 <= t <= 32:
            scale = 2.0 * dens
            for n, f in enumerate((fa, fr, fz)):
                weight[n, rows, :] = (scale * f)[:, :128]
    for t in range(1, 33):
        here, ahead, behind, rows = pl.ds(8 * t, 8), pl.ds(8 * t + 1, 8), pl.ds(8 * t - 1, 8), pl.ds(8 * t - 8, 8)
        ha, hr, hz = hfield[0, here, :], hfield[1, here, :], hfield[2, here, :]
        before = wide[6, here, :]
        (rel,) = lookup(planes[3, rows, :], (reluct,))
        hr_before = rel * ((lnext(before) - before)[:, :128] - (pot[2, 0, rows, :] - planes[2, rows, :]))
        hz_before = rel * ((pot[1, 0, rows, :] - planes[1, rows, :]) - (wide[6, ahead, :] - before)[:, :128])
        ca = ((lprev(hr) - hr) - (hfield[2, behind, :] - hz))[:, :128]
        cr = (hz_before - hz[:, :128]) - (lprev(ha) - ha)[:, :128]
        cz = (hfield[0, behind, :] - ha)[:, :128] - (hr_before - hr[:, :128])
        (sigma,) = lookup(region[rows, :], (eddy,))
        for n, c in enumerate((ca, cr, cz)):
            misfit[n, 0, rows, :] = c + sigma * pot[n, 0, rows, :] - current[n, 0, rows, :]


def heat_kernel(
    got, prior, goal, from_next, from_prev, sides,
    plane, axial, storage, out,
    kin, kax, cap, pri, sens, src, coef, base, temp0, temp1, adj0, adj1,
):
    low = sub_low()

    def join(tiles, ends):
        return jnp.concatenate([jnp.concatenate(tiles, axis=0), jnp.concatenate(ends, axis=0)], axis=1)

    def gather(g, carry):
        inner = sides[NA + g]
        outer = jnp.where(low, from_next[NA + g], from_prev[NA + g])
        for u in range(8):
            a = 8 * g + u
            tiles = [got[a, pl.ds(8 * c, 8), :] for c in range(4)]
            side = got[a, pl.ds(32, 8), :]
            ends = [take(side, c) for c in range(4)]
            src[a] = join(tiles[:2], ends[:2])
            kin[a], kax[a], cap[a] = lookup(join(tiles[2:], ends[2:]), (plane, axial, storage))
            held = heat_tiles(prior, goal, from_next, from_prev, a)
            pri[a] = join(held[0], [take(inner, 2 * u), take(outer, 2 * u)])
            sens[a] = join(held[1], [take(inner, 2 * u + 1), take(outer, 2 * u + 1)])
        return carry

    lax.fori_loop(0, NA // 8, gather, 0)

    def prepare(a, carry):
        up = (a + 1) & (NA - 1)
        down = (a - 1) & (NA - 1)
        kp, ka, c = kin[a], kax[a], cap[a]
        source = c * pri[a] + src[a]
        w = [
            0.5 * (kp + kin[up]), 0.5 * (kp + kin[down]),
            0.5 * (kp + rnext(kp)), 0.5 * (kp + rprev(kp)),
            0.5 * (ka + lnext(ka)), 0.5 * (ka + lprev(ka)),
        ]
        total = c + (((((w[0] + w[1]) + w[2]) + w[3]) + w[4]) + w[5])
        inside = c > 0.0
        inv = jnp.where(inside, 1.0 / jnp.where(inside, total, 1.0), 0.0)
        for n in range(6):
            coef[n, a] = inv * w[n]
        base[0, a] = inv * source
        first = inv * sens[a]
        base[1, a] = first
        adj0[a] = first
        return carry

    lax.fori_loop(0, NA, prepare, 0, unroll=16)

    def relax(field, a, c, b):
        up = (a + 1) & (NA - 1)
        down = (a - 1) & (NA - 1)
        v = field[a]
        total = b + c[0] * field[up] + c[1] * field[down]
        total = total + c[2] * rnext(v) + c[3] * rprev(v)
        return total + c[4] * lnext(v) + c[5] * lprev(v)

    temps = [pri, temp0, temp1, temp0, temp1]
    adjs = [None, adj0, adj1, adj0, adj1]
    for sweep in range(SWEEPS):

        def step(a, carry, sweep=sweep):
            c = [coef[n, a] for n in range(6)]
            t = relax(temps[sweep], a, c, base[0, a])
            if sweep == SWEEPS - 1:
                out[a, pl.ds(0, 8), :] = t[:8, :128]
            else:
                temps[sweep + 1][a] = t
            if sweep > 0:
                s = relax(adjs[sweep], a, c, base[1, a])
                if sweep == SWEEPS - 1:
                    out[a, pl.ds(8, 8), :] = s[:8, :128]
                else:
                    adjs[sweep + 1][a] = s
            return carry

        lax.fori_loop(0, NA, step, 0, unroll=32)


def finish_kernel(got, weight, dual, state):
    def step(j, carry):
        at = pl.ds(pl.multiple_of(8 * j, 8), 8)
        state[0, at, :] = got[j, pl.ds(0, 8), :]
        adjoint = got[j, pl.ds(8, 8), :]
        for f in range(3):
            dual[f, 0, at, :] = weight[f, at, :] * adjoint
        return carry

    lax.fori_loop(0, NA, step, 0, unroll=8)


def body(
    magnetic_vector_field,
    imposed_current_density,
    fixed_material_map,
    spinning_material_map,
    slab_slide_offsets,
    inverse_permeability,
    electric_conductance,
    core_dissipation_coefficient,
    inplane_thermal_conductance,
    through_plane_conductance,
    thermal_storage,
    prior_thermal_state,
    goal_sensitivity,
):
    rows = lax.axis_size("section") * lax.axis_size("azim")
    chain = ("section", "azim")
    onward = [(i, i + 1) for i in range(rows - 1)]
    backward = [(i + 1, i) for i in range(rows - 1)]
    from_after = [((i + 1) % NA, i) for i in range(NA)]
    from_before = [(i, (i + 1) % NA) for i in range(NA)]

    offsets = slab_slide_offsets.reshape(1, 128)
    maps = (fixed_material_map, spinning_material_map, offsets)
    row_edge, edge, ring, planes = pl.pallas_call(
        send_kernel,
        out_shape=tuple(pltpu.VMEM(d, F32) for d in ((4, 8, 128), (12, 8, 128), (2, 256, 128), (4, 256, 128))),
        in_specs=[HBM] * 6,
        out_specs=(VM,) * 4,
        scratch_shapes=[
            pltpu.VMEM((3, 1, 256, 128), F32),
            pltpu.VMEM((1, 256, 128), jnp.int32),
            pltpu.VMEM((NA, 128), jnp.int32),
            pltpu.VMEM((1, 128), jnp.int32),
            pltpu.VMEM((NA, 8, 128), F32),
            pltpu.VMEM((NA, 8, 128), F32),
            pltpu.VMEM((256, 128), F32),
            pltpu.SemaphoreType.DMA((6,)),
        ],
        compiler_params=params(56),
        name="send",
    )(magnetic_vector_field, *maps, prior_thermal_state, goal_sensitivity)
    across = lax.ppermute(row_edge, "section", [(0, 1), (1, 0)])
    frame = pl.pallas_call(
        frame_kernel, out_shape=struct(16, 8, 128), in_specs=[VM] * 2, out_specs=VM,
        compiler_params=params(8), name="frame",
    )(edge, across)
    frame, ring, planes = lax.optimization_barrier((frame, ring, planes))
    ring = lax.ppermute(ring, "azim", from_after)
    planes = lax.ppermute(planes, "azim", from_before)
    core = lax.ppermute(frame, "axial", [(0, 1), (1, 0), (2, 3), (3, 2)])
    far = lax.ppermute(frame, "axial", [(1, 2), (2, 1)])
    halo, heat_down, heat_up = pl.pallas_call(
        halo_kernel,
        out_shape=(struct(16, 8, 128), struct(NA + 4, 8, 128), struct(NA + 4, 8, 128)),
        in_specs=[VM] * 5,
        out_specs=(VM,) * 3,
        compiler_params=params(8),
        name="halo",
    )(frame, core, far, prior_thermal_state, goal_sensitivity)
    halo_after = lax.ppermute(halo, "azim", from_after)
    block = (magnetic_vector_field, *maps, halo, ring, halo_after)
    payload = pl.pallas_call(
        magnetic_kernel,
        out_shape=pltpu.VMEM((NA, 40, 128), F32),
        in_specs=[VM] * 7 + [SM],
        out_specs=VM,
        scratch_shapes=[
            pltpu.VMEM((6, 280, 256), F32),
            pltpu.VMEM((34, 8, 256), F32),
            pltpu.VMEM((256, 128), F32),
        ],
        compiler_params=params(24),
        name="magnetic",
    )(*block, core_dissipation_coefficient)
    halo_before = lax.ppermute(halo, "azim", from_before)
    payload, planes, halo_before = lax.optimization_barrier((payload, planes, halo_before))
    got = lax.all_to_all(payload, "azim", split_axis=0, concat_axis=0, tiled=True)
    heat_prev = lax.ppermute(heat_up, chain, onward)
    heat_next = lax.ppermute(heat_down, chain, backward)
    misfit, weight = pl.pallas_call(
        curl_kernel,
        out_shape=(struct(3, 1, 256, 128), struct(3, 256, 128)),
        in_specs=[VM] * 10 + [SM] * 3,
        out_specs=(VM, VM),
        scratch_shapes=[
            pltpu.VMEM((7, 280, 256), F32),
            pltpu.VMEM((3, 272, 256), F32),
            pltpu.VMEM((256, 128), F32),
        ],
        compiler_params=params(24),
        cost_estimate=pl.CostEstimate(flops=10_000_000, bytes_accessed=10_000_000, transcendentals=0),
        name="curl",
    )(
        *block, planes, halo_before, imposed_current_density,
        inverse_permeability, electric_conductance, core_dissipation_coefficient,
    )
    got, misfit, weight = lax.optimization_barrier((got, misfit, weight))
    wide = pltpu.VMEM((NA, 16, 256), F32)
    result = pl.pallas_call(
        heat_kernel,
        out_shape=pltpu.VMEM((NA, 16, 128), F32),
        in_specs=[VM] * 6 + [SM] * 3,
        out_specs=VM,
        scratch_shapes=[
            wide, wide, wide, wide, wide, wide,
            pltpu.VMEM((6, NA, 16, 256), F32),
            pltpu.VMEM((2, NA, 16, 256), F32),
            wide, wide, wide, wide,
        ],
        compiler_params=params(32),
        cost_estimate=pl.CostEstimate(flops=20_000_000, bytes_accessed=20_000_000, transcendentals=0),
        name="heat",
    )(
        got, prior_thermal_state, goal_sensitivity, heat_next, heat_prev, heat_down,
        inplane_thermal_conductance, through_plane_conductance, thermal_storage,
    )
    back = lax.all_to_all(result, "azim", split_axis=0, concat_axis=0, tiled=True)
    dual, state = pl.pallas_call(
        finish_kernel,
        out_shape=(struct(3, 1, 256, 128), struct(1, 256, 128)),
        in_specs=[VM] * 2,
        out_specs=(VM,) * 2,
        compiler_params=params(16),
        name="finish",
    )(back, weight)
    return misfit, dual, state


def solution(mesh):
    in_specs = (
        P(None, "azim", "section", "axial"),
        P(None, "azim", "section", "axial"),
        P("azim", "section", "axial"),
        P(),
        P("axial"),
        P(),
        P(),
        P(),
        P(),
        P(),
        P(),
        P(None, ("section", "azim"), "axial"),
        P(None, ("section", "azim"), "axial"),
    )
    out_specs = (
        P(None, "azim", "section", "axial"),
        P(None, "azim", "section", "axial"),
        P("azim", "section", "axial"),
    )
    return jax.shard_map(body, mesh=mesh, in_specs=in_specs, out_specs=out_specs, check_vma=False)
```
